512 devices in a mesh: prow: 32 (over x, y, core), hrow: 16 (over z).
Axes of the slice: x: 4, y: 4, z: 16, core: 2. Of those that a mesh axis runs over, the one named last changes fastest.
Arguments:
- packet: float32 [20480, 512], P(('prow', 'hrow')), may hold values from -20 to 20
- header: float32 [20480, 512], P(('hrow', 'prow')), may hold values from -20 to 20
- partner: int32 [20480], replicated, may hold values from 0 to 20479, as said below
Outputs:
- loss: float32 [], replicated
- packet_grad: float32 [20480, 512], P(('prow', 'hrow'))
- header_grad: float32 [20480, 512], P(('hrow', 'prow'))
The draws below stay inside these ranges and needn't reach their ends.
Inputs may be any that keep to these rules, and one draw needn't show every extreme that they name: `partner`: each header row is matched by exactly one packet row.
All inputs are finite; a program needn't handle non-finite values.
Results may differ from the reference program's by a relative error of at most 0.0003.
Values sent between devices are 32-bit elements; how exact they have to be, the bound alone decides.
No kernel may reach another device: no remote copies, remote signals or barrier semaphores. Data moves between devices by JAX's collectives and lax.ppermute only.
A program may use at most 64 MiB of HBM per device.

```python
import math
import jax
import jax.numpy as jnp
from jax import lax

D = 512
BATCH = 20480


def base_rows(key):
    noise = jax.random.normal(jax.random.fold_in(key, 101), (BATCH, D), jnp.float32)
    noise = jnp.clip(noise, -4.5, 4.5)
    flags = jax.random.uniform(jax.random.fold_in(key, 102), (BATCH, 1), jnp.float32)
    offset = jax.random.randint(jax.random.fold_in(key, 103), (), 1, BATCH)
    nearby = jnp.roll(noise, offset, axis=0)
    return jnp.where(flags < 0.25, 0.8 * nearby + 0.6 * noise, noise)


def pair_order(key):
    return jax.random.permutation(jax.random.fold_in(key, 104), BATCH).astype(jnp.int32)


def draw_partner(key, part):
    order = pair_order(key)
    return order


def draw_packet(key, part):
    values = base_rows(key)
    return values


def draw_header(key, part):
    values = base_rows(key)
    order = pair_order(key)
    key = jax.random.fold_in(key, 7)
    strength = jax.random.uniform(jax.random.fold_in(key, 1), (BATCH, 1), jnp.float32, 0.45, 0.85)
    noise = jnp.clip(jax.random.normal(jax.random.fold_in(key, 2), (BATCH, D), jnp.float32), -4.5, 4.5)
    mixed = strength * values + jnp.sqrt(1.0 - strength * strength) * noise
    return jnp.zeros((BATCH, D), jnp.float32).at[order].set(mixed)


def setup_inputs(seed: int = 0) -> dict:
    arg_keys = jax.random.split(jax.random.key(seed), 4)
    packet = draw_packet(jax.random.fold_in(arg_keys[3], 71), 0)
    header = draw_header(jax.random.fold_in(arg_keys[3], 71), 0)
    partner = draw_partner(jax.random.fold_in(arg_keys[3], 71), 0)
    return dict(packet=packet, header=header, partner=partner)


inv_temp = 1.0 / 0.07
eps_norm = 1e-06

def unit_rows(values):
    norms = jnp.sqrt(lax.optimization_barrier(jnp.sum(values * values, axis=1, keepdims=True)) + eps_norm)
    return (values / norms, norms)

def reference(packet, header, partner):
    punit, pnorm = unit_rows(packet)
    hunit, hnorm = unit_rows(header)
    block = math.gcd(BATCH, 512)
    count = BATCH // block
    pblocks = punit.reshape(count, block, D)
    parts = partner.reshape(count, block)
    columns = jnp.arange(BATCH, dtype=jnp.int32)

    def first(colacc, rows_here):
        scores = jnp.dot(rows_here, hunit.T, precision=lax.Precision.HIGHEST, preferred_element_type=jnp.float32) * inv_temp
        expo = jnp.exp(scores - inv_temp)
        return (colacc + lax.optimization_barrier(jnp.sum(expo, axis=0)), lax.optimization_barrier(jnp.sum(expo, axis=1)))
    cols, rows = lax.scan(first, jnp.zeros((BATCH,), jnp.float32), pblocks)
    matched = jnp.take(hunit, partner, axis=0)
    positive = inv_temp * jnp.sum(punit * matched)
    loss = inv_temp + (jnp.sum(jnp.log(rows)) + jnp.sum(jnp.log(cols)) - 2.0 * positive) / (2.0 * BATCH)
    coeff = 1.0 / (2.0 * BATCH)

    def second(hacc, items):
        rows_here, totals, wanted = items
        scores = jnp.dot(rows_here, hunit.T, precision=lax.Precision.HIGHEST, preferred_element_type=jnp.float32) * inv_temp
        expo = jnp.exp(scores - inv_temp)
        match = (wanted[:, None] == columns[None, :]).astype(jnp.float32)
        dscores = coeff * (expo / totals[:, None] + expo / cols[None, :] - 2.0 * match)
        gp = jnp.dot(dscores, hunit, precision=lax.Precision.HIGHEST, preferred_element_type=jnp.float32) * inv_temp
        gh = jnp.dot(dscores.T, rows_here, precision=lax.Precision.HIGHEST, preferred_element_type=jnp.float32) * inv_temp
        return (hacc + gh, gp)
    ghunit, gpblocks = lax.scan(second, jnp.zeros((BATCH, D), jnp.float32), (pblocks, rows, parts))
    gpunit = gpblocks.reshape(BATCH, D)
    packet_grad = (gpunit - punit * lax.optimization_barrier(jnp.sum(punit * gpunit, axis=1, keepdims=True))) / pnorm
    header_grad = (ghunit - hunit * lax.optimization_barrier(jnp.sum(hunit * ghunit, axis=1, keepdims=True))) / hnorm
    return (loss, packet_grad, header_grad)
```

```python
import functools

import jax
import jax.numpy as jnp
import numpy as np
from jax import lax
from jax.experimental import pallas as pl
from jax.experimental.pallas import tpu as pltpu
from jax.sharding import Mesh, PartitionSpec as P

inv_temp = 1.0 / 0.07
eps_norm = 1e-06
NX, NY, NC, NZ = 4, 4, 2, 16
ALL = ("x", "y", "core", "z")
B = 40
D = 512
ROWS = NC * NZ * B
COLS = NX * NY * B
BATCH = NX * NY * ROWS
PLACES = (0, 1, -1, 2)
VMEM_LIMIT = 48 * 2**20


def take_from(value, dx=0, dy=0, dz=0, dc=0):
    pairs = []
    for x in range(NX):
        for y in range(NY):
            for c in range(NC):
                s = 1 - 2 * c
                for z in range(NZ):
                    sx, sy, sz = (x + s * dx) % NX, (y + s * dy) % NY, (z + s * dz) % NZ
                    src = ((sx * NY + sy) * NC + (c ^ dc)) * NZ + sz
                    pairs.append((src, ((x * NY + y) * NC + c) * NZ + z))
    return lax.ppermute(value, ALL, pairs)


def row_blocks(c, z):
    s = 1 - 2 * c
    o = 1 - c

    def at(core, k):
        return core * NZ + lax.rem(z + s * k + 2 * NZ, NZ)

    found = [("own", None, at(c, 0)), ("oth", None, at(o, 0))]
    for k in range(1, 8):
        found.append((f"n{k}", 0, at(c, -k)))
        found.append((f"n{k}", 1, at(o, -k)))
    found.append(("n8", None, at(c, -8)))
    for k in range(1, 5):
        found.append(("ma", 2 * (k - 1), at(o, k)))
        found.append(("ma", 2 * (k - 1) + 1, at(c, k)))
    for k in range(5, 8):
        found.append(("mb", 2 * (k - 5), at(o, k)))
        found.append(("mb", 2 * (k - 5) + 1, at(c, k)))
    found.append(("mb", 6, at(o, 8)))
    return found


ROW_NAMES = ("own", "oth", "n1", "n2", "n3", "n4", "n5", "n6", "n7", "n8", "ma", "mb")
ROW_SHAPES = ((B, D),) * 2 + ((2, B, D),) * 7 + ((B, D), (8, B, D), (7, B, D))


def col_blocks(x, y, c):
    s = 1 - 2 * c
    found = []
    for i, dy in enumerate(PLACES):
        for j, dx in enumerate(PLACES):
            bx = lax.rem(x + s * dx + NX, NX)
            by = lax.rem(y + s * dy + NY, NY)
            found.append((i, j, bx * NY + by))
    return found


def block_at(ref, block):
    return ref.at[pl.ds(pl.multiple_of(block * B, 8), B), :]


def split(value):
    high = value.astype(jnp.bfloat16)
    return high, (value - high.astype(jnp.float32)).astype(jnp.bfloat16)


def product(a_high, a_low, b_high, b_low, dims):
    dot = functools.partial(
        lax.dot_general, dimension_numbers=(dims, ((), ())), preferred_element_type=jnp.float32
    )
    return dot(a_high, b_high) + (dot(a_high, b_low) + dot(a_low, b_high))


def eye():
    return lax.broadcasted_iota(jnp.int32, (128, 128), 0) == lax.broadcasted_iota(
        jnp.int32, (128, 128), 1
    )


def to_lanes(column):
    return jnp.sum(jnp.where(eye(), column, 0.0), axis=0, keepdims=True)


def to_rows(lanes):
    return jnp.sum(jnp.where(eye(), lanes, 0.0), axis=1, keepdims=True)


STEP = 256


def scores_kernel(place, ids, wanted, *refs):
    rows_in = dict(zip(ROW_NAMES, refs[:12]))
    cols_in = refs[12:16]
    expo, ph, plow, hh, hlow, row_sums, col_sums, punit, hunit = refs[16:]
    x, y, c, z = place[0], place[1], place[2], place[3]

    def unit(v):
        return v * (1.0 / jnp.sqrt(jnp.sum(v * v, axis=1, keepdims=True) + eps_norm))

    for i, j, block in col_blocks(x, y, c):
        block_at(hunit, block)[...] = unit(cols_in[i][j])
    for name, index, block in row_blocks(c, z):
        v = rows_in[name][...] if index is None else rows_in[name][index]
        block_at(punit, block)[...] = unit(v)
    hh[...], hlow[...] = split(hunit[...])
    places = ids[...]

    def step(i, carry):
        total, positive = carry
        here = pl.ds(pl.multiple_of(i * STEP, STEP), STEP)
        high, low = split(punit[here, :])
        ph[here, :] = high
        plow[here, :] = low
        scores = product(high, low, hh[...], hlow[...], ((1,), (1,))) * inv_temp
        e = jnp.exp(scores - inv_temp)
        expo[here, :] = e
        sums = jnp.sum(e, axis=1, keepdims=True)
        for k in range(STEP // 128):
            row_sums[pl.ds(i * (STEP // 128) + k, 1), :] = to_lanes(sums[k * 128 : (k + 1) * 128])
        match = wanted[here, :] == places
        total = total + jnp.sum(e.reshape(STEP // 8, 8, COLS), axis=0)
        positive = positive + jnp.sum(
            jnp.where(match, scores, 0.0).reshape(STEP // 8, 8, COLS), axis=0
        )
        return total, positive

    zero = jnp.zeros((8, COLS), jnp.float32)
    row_sums[...] = jnp.zeros_like(row_sums)
    total, positive = lax.fori_loop(0, ROWS // STEP, step, (zero, zero))
    total = jnp.sum(total, axis=0, keepdims=True)
    positive = jnp.sum(positive, axis=0, keepdims=True)
    col_sums[...] = jnp.zeros_like(col_sums)
    for k in range(COLS // 128):
        col_sums[pl.ds(k, 1), :] = total[:, k * 128 : (k + 1) * 128]
    row_sums[pl.ds(10, 1), :] = sum(positive[:, k * 128 : (k + 1) * 128] for k in range(COLS // 128))


def packet_kernel(place, ids, wanted, rows_all, cols_all, expo, hh, hlow, *refs):
    rows_out = dict(zip(ROW_NAMES, refs[:12]))
    dh, dlow, grads = refs[12:]
    c, z = place[2], place[3]
    scale = inv_temp / (2.0 * BATCH)
    rows = jnp.sum(rows_all[...], axis=0)
    cols = jnp.sum(cols_all[...], axis=0)
    row_inv = scale / rows[:10]
    col_inv = jnp.concatenate([scale / cols[k : k + 1] for k in range(COLS // 128)], axis=1)
    places = ids[...]
    for i in range(ROWS // STEP):
        here = pl.ds(i * STEP, STEP)
        per_row = jnp.concatenate(
            [to_rows(row_inv[i * 2 + k : i * 2 + k + 1]) for k in range(STEP // 128)], axis=0
        )
        match = wanted[here, :] == places
        d = expo[here, :] * (per_row + col_inv) - jnp.where(match, 2.0 * scale, 0.0)
        high, low = split(d)
        dh[here, :] = high
        dlow[here, :] = low
        grads[here, :] = product(high, low, hh[...], hlow[...], ((1,), (0,)))
    for name, index, block in row_blocks(c, z):
        v = block_at(grads, block)[...]
        if index is None:
            rows_out[name][...] = v
        else:
            rows_out[name][index] = v


def header_kernel(place, dh, dlow, ph, plow, *refs):
    cols_out = refs[:4]
    grads = refs[4]
    x, y, c = place[0], place[1], place[2]
    for k in range(COLS // 128):
        here = pl.ds(k * 128, 128)
        grads[here, :] = product(dh[:, here], dlow[:, here], ph[...], plow[...], ((0,), (0,)))
    for i, j, block in col_blocks(x, y, c):
        cols_out[i][j] = block_at(grads, block)[...]


def in_vmem(count):
    return [pl.BlockSpec(memory_space=pltpu.VMEM)] * count


def call(kernel, operands, outs, scratch, flops):
    return pl.pallas_call(
        kernel,
        in_specs=[pl.BlockSpec(memory_space=pltpu.SMEM)] + in_vmem(len(operands) - 1),
        out_specs=in_vmem(len(outs)),
        out_shape=outs,
        scratch_shapes=scratch,
        compiler_params=pltpu.CompilerParams(vmem_limit_bytes=VMEM_LIMIT),
        cost_estimate=pl.CostEstimate(flops=flops, bytes_accessed=8 * 2**20, transcendentals=0),
    )(*operands)


def f32(*shape):
    return jax.ShapeDtypeStruct(shape, jnp.float32)


def b16(*shape):
    return jax.ShapeDtypeStruct(shape, jnp.bfloat16)


def unit_rows(values):
    norms = jnp.sqrt(jnp.sum(values * values, axis=1, keepdims=True) + eps_norm)
    return (values / norms, norms)


def unit_back(grads, units, norms):
    return (grads - units * jnp.sum(units * grads, axis=1, keepdims=True)) / norms


def gather_packet(packet):
    oth = take_from(packet, dc=1)
    pair = jnp.stack([packet, oth])
    near = []
    for _ in range(7):
        pair = take_from(pair, dz=-1)
        near.append(pair)
    n8 = take_from(pair[0], dz=-1)
    ma = take_from(jnp.concatenate(near[:4]), dc=1)
    mb = take_from(jnp.concatenate(near[4:] + [n8[None]]), dc=1)
    return [packet, oth] + near + [n8, ma, mb]


def gather_header(header):
    xa = take_from(header, dx=1)
    xb = take_from(header, dx=-1)
    xc = take_from(xa, dx=1)
    line = jnp.stack([header, xa, xb, xc])
    ya = take_from(line, dy=1)
    yb = take_from(line, dy=-1)
    yc = take_from(ya, dy=1)
    return [line, ya, yb, yc]


def scatter_packet(parts):
    own, oth, near, n8, ma, mb = parts[0], parts[1], parts[2:9], parts[9], parts[10], parts[11]
    far = take_from(mb, dc=1)
    close = take_from(ma, dc=1)
    got = take_from(n8 + far[6], dz=1)
    acc = near[6] + far[4:6] + jnp.stack([got, jnp.zeros_like(got)])
    for k in range(6, 0, -1):
        also = far[2 * (k - 5) : 2 * (k - 4)] if k >= 5 else close[2 * (k - 1) : 2 * k]
        acc = near[k - 1] + also + take_from(acc, dz=1)
    got = take_from(acc, dz=1)
    return own + got[0] + take_from(oth + got[1], dc=1)


def scatter_header(parts):
    line, ya, yb, yc = parts
    line = line + take_from(ya + take_from(yc, dy=-1), dy=-1) + take_from(yb, dy=1)
    return line[0] + take_from(line[1] + take_from(line[3], dx=-1), dx=-1) + take_from(line[2], dx=1)


def per_device(packet, header, partner):
    x, y, c, z = (lax.axis_index(name) for name in ALL)
    place = jnp.stack([x, y, c, z]).astype(jnp.int32)
    lane = np.arange(COLS)
    ids = jnp.asarray((lane // B) * (NC * B) + lane % B, jnp.int32)[None, :]
    ids = ids + (z * (NX * NY * NC * B) + c * B).astype(jnp.int32)
    wanted = lax.dynamic_slice_in_dim(partner, (x * NY + y) * ROWS, ROWS)[:, None]

    rows_in = gather_packet(packet)
    cols_in = gather_header(header)
    flops = 2 * 3 * ROWS * COLS * D
    expo, ph, plow, hh, hlow, row_part, col_part = call(
        scores_kernel,
        [place, ids, wanted] + rows_in + cols_in,
        [f32(ROWS, COLS), b16(ROWS, D), b16(ROWS, D), b16(COLS, D), b16(COLS, D), f32(16, 128), f32(8, 128)],
        [pltpu.VMEM((ROWS, D), jnp.float32), pltpu.VMEM((COLS, D), jnp.float32)],
        flops,
    )
    rows_all = lax.all_to_all(jnp.broadcast_to(row_part, (NC * NZ, 16, 128)), ("core", "z"), 0, 0)
    rows = jnp.sum(rows_all, axis=0)
    row_term = jnp.sum(jnp.log(rows[:10])) - 2.0 * jnp.sum(rows[10])
    last = lax.broadcasted_iota(jnp.int32, (8, 128), 0) == 7
    col_part = jnp.where(last, row_term, col_part)
    cols_all = lax.all_to_all(jnp.broadcast_to(col_part, (NX * NY, 8, 128)), ("x", "y"), 0, 0)
    cols = jnp.sum(cols_all, axis=0)
    col_term = jnp.sum(jnp.log(cols[: COLS // 128]))
    col_terms = lax.all_to_all(
        jnp.broadcast_to(col_term, (NC * NZ, 8, 128)), ("core", "z"), 0, 0
    )
    loss = inv_temp + (cols[7, 0] + jnp.sum(col_terms[:, 0, 0])) / (2.0 * BATCH)

    outs = call(
        packet_kernel,
        [place, ids, wanted, rows_all, cols_all, expo, hh, hlow],
        [f32(*shape) for shape in ROW_SHAPES] + [b16(ROWS, COLS), b16(ROWS, COLS)],
        [pltpu.VMEM((ROWS, D), jnp.float32)],
        flops,
    )
    dh, dlow = outs[12:]
    gh_parts = call(
        header_kernel,
        [place, dh, dlow, ph, plow],
        [f32(4, B, D)] * 4,
        [pltpu.VMEM((COLS, D), jnp.float32)],
        flops,
    )
    gpunit = scatter_packet(outs[:12])
    ghunit = scatter_header(gh_parts)
    punit, pnorm = unit_rows(packet)
    hunit, hnorm = unit_rows(header)
    packet_grad = unit_back(gpunit, punit, pnorm)
    header_grad = unit_back(ghunit, hunit, hnorm)
    return (loss, packet_grad, header_grad)


def solution(mesh):
    mesh = Mesh(mesh.devices.reshape(NX, NY, NC, NZ), ALL)
    by_packet, by_header = P(ALL, None), P(("z", "x", "y", "core"), None)
    return jax.shard_map(
        per_device,
        mesh=mesh,
        in_specs=(by_packet, by_header, P()),
        out_specs=(P(), by_packet, by_header),
        check_vma=False,
    )
```

```python
import functools

import jax
import jax.numpy as jnp
import numpy as np
from jax import lax
from jax.experimental import pallas as pl
from jax.experimental.pallas import tpu as pltpu
from jax.sharding import Mesh, PartitionSpec as P

inv_temp = 1.0 / 0.07
eps_norm = 1e-06
NX, NY, NC, NZ = 4, 4, 2, 16
NH, NL = 4, 4
ALL = ("x", "y", "core", "zh", "zl")
B = 40
D = 512
ROWS = NX * NC * NL * B
COLS = NY * NH * B
BATCH = NX * NY * NC * NZ * B
E = B + 8
GROUP = 4 * B + 8
PLACES = (0, 1, -1, 2)
VMEM_LIMIT = 48 * 2**20


def permute(value, source):
    pairs = []
    for x in range(NX):
        for y in range(NY):
            for c in range(NC):
                for z in range(NZ):
                    sx, sy, sc, sz = source(x, y, c, z)
                    src = (((sx % NX) * NY + sy % NY) * NC + sc) * NZ + sz
                    pairs.append((src, ((x * NY + y) * NC + c) * NZ + z))
    return lax.ppermute(value, ALL, pairs)


def along_x(value, step):
    return permute(value, lambda x, y, c, z: (x + (1 - 2 * c) * step, y, c, z))


def along_y(value, step):
    return permute(value, lambda x, y, c, z: (x, y + (1 - 2 * c) * step, c, z))


def along_zh(value, step):
    return permute(value, lambda x, y, c, z: (x, y, c, (z + (1 - 2 * c) * NL * step) % NZ))


def swap_zl(value, bit):
    return permute(value, lambda x, y, c, z: (x, y, c, z ^ bit))


def swap_core(value):
    return permute(value, lambda x, y, c, z: (x, y, c ^ 1, z))


def row_blocks(x, c, zl):
    found = []
    for other in range(2):
        core = c if other == 0 else 1 - c
        sign = 1 - 2 * core
        for j, dx in enumerate(PLACES):
            bx = lax.rem(x + sign * dx + NX, NX)
            for k, flip in enumerate((0, 2, 1, 3)):
                found.append((other, j, k, (bx * NC + core) * NL + (zl ^ flip)))
    return found


def col_blocks(y, c, zh):
    s = 1 - 2 * c
    found = []
    for j, dy in enumerate(PLACES):
        by = lax.rem(y + s * dy + NY, NY)
        for k, dz in enumerate(PLACES):
            found.append((j, k, lax.rem(zh + s * dz + NH, NH) * NY + by))
    return found


def block_at(ref, block):
    return ref.at[pl.ds(pl.multiple_of(block * B, 8), B), :]


def split(value):
    high = value.astype(jnp.bfloat16)
    return high, (value - high.astype(jnp.float32)).astype(jnp.bfloat16)


def product(a_high, a_low, b_high, b_low, dims):
    dot = functools.partial(
        lax.dot_general, dimension_numbers=(dims, ((), ())), preferred_element_type=jnp.float32
    )
    return dot(a_high, b_high) + (dot(a_high, b_low) + dot(a_low, b_high))


def eye():
    return lax.broadcasted_iota(jnp.int32, (128, 128), 0) == lax.broadcasted_iota(
        jnp.int32, (128, 128), 1
    )


def to_lanes(column):
    return jnp.sum(jnp.where(eye(), column, 0.0), axis=0, keepdims=True)


def to_rows(lanes):
    return jnp.sum(jnp.where(eye(), lanes, 0.0), axis=1, keepdims=True)


STEP = 256


def scores_kernel(place, ids, wanted, *refs):
    rows_in, others_in, cols_in = refs[:4], refs[4], refs[5:9]
    expo, ph, plow, hh, hlow, row_sums, col_sums, punit, hunit = refs[9:]
    x, y, c, zh, zl = (place[k] for k in range(5))

    def unit(v):
        return v * (1.0 / jnp.sqrt(jnp.sum(v * v, axis=1, keepdims=True) + eps_norm))

    for j, k, block in col_blocks(y, c, zh):
        block_at(hunit, block)[...] = unit(cols_in[j][k])
    for other, j, k, block in row_blocks(x, c, zl):
        block_at(punit, block)[...] = unit(others_in[j, k] if other else rows_in[j][k])
    hh[...], hlow[...] = split(hunit[...])
    places = ids[...]

    def step(i, carry):
        total, positive = carry
        here = pl.ds(pl.multiple_of(i * STEP, STEP), STEP)
        high, low = split(punit[here, :])
        ph[here, :] = high
        plow[here, :] = low
        scores = product(high, low, hh[...], hlow[...], ((1,), (1,))) * inv_temp
        e = jnp.exp(scores - inv_temp)
        expo[here, :] = e
        sums = jnp.sum(e, axis=1, keepdims=True)
        for k in range(STEP // 128):
            lanes = pl.ds(pl.multiple_of(i * STEP + k * 128, 128), 128)
            row_sums[:, lanes] = to_lanes(sums[k * 128 : (k + 1) * 128])
        match = wanted[here, :] == places
        total = total + jnp.sum(e.reshape(STEP // 8, 8, COLS), axis=0)
        positive = positive + jnp.sum(
            jnp.where(match, scores, 0.0).reshape(STEP // 8, 8, COLS), axis=0
        )
        return total, positive

    zero = jnp.zeros((8, COLS), jnp.float32)
    total, positive = lax.fori_loop(0, ROWS // STEP, step, (zero, zero))
    col_sums[...] = jnp.sum(total, axis=0, keepdims=True)
    positive = jnp.sum(positive, axis=0, keepdims=True)
    row_sums[:, ROWS:] = sum(positive[:, k * 128 : (k + 1) * 128] for k in range(COLS // 128))


def packet_kernel(place, ids, wanted, rows, cols, expo, hh, hlow, mine, others, row_term, dh, dlow, grads):
    x, y, c, zh, zl = (place[k] for k in range(5))
    scale = inv_temp / (2.0 * BATCH)
    rows = jnp.sum(rows[...], axis=0, keepdims=True)
    cols = jnp.sum(cols[...], axis=0, keepdims=True)
    row_term[...] = jnp.zeros_like(row_term) + (
        jnp.sum(jnp.log(rows[:, :ROWS])) - 2.0 * jnp.sum(rows[:, ROWS:])
    )
    col_term = jnp.sum(jnp.log(cols))
    row_inv = scale / rows[:, :ROWS]
    col_inv = scale / cols
    places = ids[...]
    for i in range(ROWS // STEP):
        here = pl.ds(i * STEP, STEP)
        per_row = jnp.concatenate(
            [to_rows(row_inv[:, k : k + 128]) for k in range(i * STEP, (i + 1) * STEP, 128)], axis=0
        )
        match = wanted[here, :] == places
        d = expo[here, :] * (per_row + col_inv) - jnp.where(match, 2.0 * scale, 0.0)
        high, low = split(d)
        dh[here, :] = high
        dlow[here, :] = low
        grads[here, :] = product(high, low, hh[...], hlow[...], ((1,), (0,)))
    for other, j, k, block in row_blocks(x, c, zl):
        out = others if other else mine
        out[j, k * B : (k + 1) * B, :] = block_at(grads, block)[...]
    for out in (mine, others):
        out[:, 4 * B :, :] = jnp.zeros((4, 8, D), jnp.float32) + col_term


def header_kernel(place, dh, dlow, ph, plow, row_term, out, grads):
    x, y, c, zh, zl = (place[k] for k in range(5))
    for k in range(COLS // 128):
        here = pl.ds(k * 128, 128)
        grads[here, :] = product(dh[:, here], dlow[:, here], ph[...], plow[...], ((0,), (0,)))
    for j, k, block in col_blocks(y, c, zh):
        out[j, k * E : k * E + B, :] = block_at(grads, block)[...]
        out[j, k * E + B : (k + 1) * E, :] = row_term[...]


def in_vmem(count):
    return [pl.BlockSpec(memory_space=pltpu.VMEM)] * count


def call(kernel, operands, outs, scratch, flops):
    return pl.pallas_call(
        kernel,
        in_specs=[pl.BlockSpec(memory_space=pltpu.SMEM)] + in_vmem(len(operands) - 1),
        out_specs=in_vmem(len(outs)),
        out_shape=outs,
        scratch_shapes=scratch,
        compiler_params=pltpu.CompilerParams(vmem_limit_bytes=VMEM_LIMIT),
        cost_estimate=pl.CostEstimate(flops=flops, bytes_accessed=8 * 2**20, transcendentals=0),
    )(*operands)


def f32(*shape):
    return jax.ShapeDtypeStruct(shape, jnp.float32)


def b16(*shape):
    return jax.ShapeDtypeStruct(shape, jnp.bfloat16)


def unit_rows(values):
    norms = jnp.sqrt(jnp.sum(values * values, axis=1, keepdims=True) + eps_norm)
    return (values / norms, norms)


def unit_back(grads, units, norms):
    return (grads - units * jnp.sum(units * grads, axis=1, keepdims=True)) / norms


def together(*values):
    return lax.optimization_barrier(values)


def gather(packet, header):
    za = along_zh(header, 1)
    zb = along_zh(header, -1)
    two = jnp.stack([packet, swap_zl(packet, 2)])
    za, two = together(za, two)
    zc = along_zh(za, 1)
    prow = jnp.concatenate([two, swap_zl(two, 1)])
    hrow = jnp.stack([header, za, zb, zc])
    hrow, prow = together(hrow, prow)
    ya, yb = along_y(hrow, 1), along_y(hrow, -1)
    xa, xb = along_x(prow, 1), along_x(prow, -1)
    ya, yb, xa = together(ya, yb, xa)
    yc, xc = together(along_y(ya, 1), along_x(xa, 1))
    rows_in = [prow, xa, xb, xc]
    return rows_in, swap_core(jnp.stack(rows_in)), [hrow, ya, yb, yc]


def scatter(mine, others, hpart):
    mine = mine + swap_core(others)
    ya = hpart[1] + along_y(hpart[3], -1)
    ya, mine = together(ya, mine)
    xa = mine[1] + along_x(mine[3], -1)
    hrow = hpart[0] + along_y(ya, -1) + along_y(hpart[2], 1)
    xa, hrow = together(xa, hrow)
    za = hrow[E : 2 * E] + along_zh(hrow[3 * E :], -1)
    prow = mine[0] + along_x(xa, -1) + along_x(mine[2], 1)
    za, prow = together(za, prow)
    two = jnp.concatenate([prow[: 2 * B], prow[4 * B :]]) + swap_zl(prow[2 * B :], 1)
    hown = hrow[:E] + along_zh(za, -1) + along_zh(hrow[2 * E : 3 * E], 1)
    got = swap_zl(two[B:], 2)
    return two[:B] + got[:B], two[2 * B, 0] + got[B, 0], hown[:B], hown[B, 0]


def per_device(packet, header, partner):
    x, y, c, zh, zl = (lax.axis_index(name) for name in ALL)
    place = jnp.stack([x, y, c, zh, zl]).astype(jnp.int32)
    lane = np.arange(COLS)
    ids = lane // (NY * B) * (NL * NX * NY * NC * B) + lane // B % NY * (NC * B) + lane % B
    ids = jnp.asarray(ids, jnp.int32)[None, :]
    ids = ids + ((zl * NX + x) * (NY * NC * B) + c * B).astype(jnp.int32)
    wanted = lax.dynamic_slice(
        partner.reshape(NX, NY, NC, NH, NL, B), [0, y, 0, zh, 0, 0], (NX, 1, NC, 1, NL, B)
    ).reshape(ROWS, 1)

    rows_in, others_in, cols_in = gather(packet, header)
    flops = 2 * 3 * ROWS * COLS * D
    expo, ph, plow, hh, hlow, rows, cols = call(
        scores_kernel,
        [place, ids, wanted] + rows_in + [others_in] + cols_in,
        [f32(ROWS, COLS), b16(ROWS, D), b16(ROWS, D), b16(COLS, D), b16(COLS, D), f32(1, ROWS + 128), f32(1, COLS)],
        [pltpu.VMEM((ROWS, D), jnp.float32), pltpu.VMEM((COLS, D), jnp.float32)],
        flops,
    )
    rows = lax.all_to_all(
        jnp.broadcast_to(rows[None], (NX * NC * NL, 1, ROWS + 128)), ("x", "core", "zl"), 0, 0
    )
    cols = lax.all_to_all(jnp.broadcast_to(cols[None], (NY * NH, 1, COLS)), ("y", "zh"), 0, 0)
    rows, cols = rows[:, 0], cols[:, 0]

    mine, others, row_term, dh, dlow = call(
        packet_kernel,
        [place, ids, wanted, rows, cols, expo, hh, hlow],
        [f32(4, GROUP, D), f32(4, GROUP, D), f32(8, D), b16(ROWS, COLS), b16(ROWS, COLS)],
        [pltpu.VMEM((ROWS, D), jnp.float32)],
        flops,
    )
    (gh_parts,) = call(
        header_kernel,
        [place, dh, dlow, ph, plow, row_term],
        [f32(4, 4 * E, D)],
        [pltpu.VMEM((COLS, D), jnp.float32)],
        flops,
    )
    gpunit, col_terms, ghunit, row_terms = scatter(mine, others, gh_parts)
    loss = inv_temp + (row_terms + col_terms) / (2.0 * BATCH)
    punit, pnorm = unit_rows(packet)
    hunit, hnorm = unit_rows(header)
    packet_grad = unit_back(gpunit, punit, pnorm)
    header_grad = unit_back(ghunit, hunit, hnorm)
    return (loss, packet_grad, header_grad)


def solution(mesh):
    mesh = Mesh(mesh.devices.reshape(NX, NY, NC, NH, NL), ALL)
    by_packet, by_header = P(ALL, None), P(("zh", "zl", "x", "y", "core"), None)
    return jax.shard_map(
        per_device,
        mesh=mesh,
        in_specs=(by_packet, by_header, P()),
        out_specs=(P(), by_packet, by_header),
        check_vma=False,
    )
```

```python
import functools

import jax
import jax.numpy as jnp
import numpy as np
from jax import lax
from jax.experimental import pallas as pl
from jax.experimental.pallas import tpu as pltpu
from jax.sharding import Mesh, PartitionSpec as P

inv_temp = 1.0 / 0.07
eps_norm = 1e-06
NX, NY, NC, NZ = 4, 4, 2, 16
NH, NL = 4, 4
ALL = ("x", "y", "core", "zh", "zl")
B = 40
D = 512
ROWS = NX * NC * NL * B
COLS = NY * NH * B
BATCH = NX * NY * NC * NZ * B
PAIR = 2 * B + 8
PLACES = (0, 1, -1, 2)
FLIPS = (0, 2, 1, 3)
VMEM_LIMIT = 48 * 2**20


def permute(value, source):
    pairs = []
    for x in range(NX):
        for y in range(NY):
            for c in range(NC):
                for z in range(NZ):
                    sx, sy, sc, sz = source(x, y, c, z)
                    src = (((sx % NX) * NY + sy % NY) * NC + sc) * NZ + sz
                    pairs.append((src, ((x * NY + y) * NC + c) * NZ + z))
    return lax.ppermute(value, ALL, pairs)


def along_xy(value, step):
    return permute(value, lambda x, y, c, z: (x + (1 - c) * step, y + c * step, c, z))


def along_z(value, flip, step):
    return permute(
        value, lambda x, y, c, z: (x, y, c, (z + NL * step) % NZ if c else z ^ flip)
    )


def swap_core(value):
    return permute(value, lambda x, y, c, z: (x, y, c ^ 1, z))


def groups():
    index = np.arange(NX * NY * NC * NZ).reshape(NX, NY, NC, NH, NL)
    found = []
    for i in range(4):
        for j in range(4):
            found.append(index[:, i, 0, j, :].reshape(-1).tolist())
            found.append(index[i, :, 1, :, j].reshape(-1).tolist())
    return found


def row_blocks(x, zl):
    found = []
    for j, dx in enumerate(PLACES):
        bx = lax.rem(x + dx + NX, NX)
        for k, flip in enumerate(FLIPS):
            for core in range(NC):
                found.append((j, k, core, (bx * NC + core) * NL + (zl ^ flip)))
    return found


def col_blocks(y, zh):
    found = []
    for j, dy in enumerate(PLACES):
        by = lax.rem(y + dy + NY, NY)
        for k, dz in enumerate(PLACES):
            found.append((j, k, lax.rem(zh + dz + NH, NH) * NY + by))
    return found


def block_at(ref, block):
    return ref.at[pl.ds(pl.multiple_of(block * B, 8), B), :]


def split(value):
    high = value.astype(jnp.bfloat16)
    return high, (value - high.astype(jnp.float32)).astype(jnp.bfloat16)


def product(a_high, a_low, b_high, b_low, dims):
    dot = functools.partial(
        lax.dot_general, dimension_numbers=(dims, ((), ())), preferred_element_type=jnp.float32
    )
    return dot(a_high, b_high) + (dot(a_high, b_low) + dot(a_low, b_high))


def eye():
    return lax.broadcasted_iota(jnp.int32, (128, 128), 0) == lax.broadcasted_iota(
        jnp.int32, (128, 128), 1
    )


def to_lanes(column):
    return jnp.sum(jnp.where(eye(), column, 0.0), axis=0, keepdims=True)


def to_rows(lanes):
    return jnp.sum(jnp.where(eye(), lanes, 0.0), axis=1, keepdims=True)


STEP = 256
SUMS = ROWS + 128


def scores_kernel(place, ids, wanted, *refs):
    mine, others = refs[:4], refs[4:8]
    expo, ph, plow, hh, hlow, keep, send, punit, hunit, row_sums = refs[8:]
    x, y, c, zh, zl = (place[k] for k in range(5))

    def unit(v):
        return v * (1.0 / jnp.sqrt(jnp.sum(v * v, axis=1, keepdims=True) + eps_norm))

    def fill(rows_in, cols_in, other):
        for j, k, block in col_blocks(y, zh):
            block_at(hunit, block)[...] = unit(cols_in[j][k, other * B : (other + 1) * B, :])
        for j, k, core, block in row_blocks(x, zl):
            block_at(punit, block)[...] = unit(rows_in[j][k, core * B : (core + 1) * B, :])

    @pl.when(c == 0)
    def _():
        fill(mine, others, 1)

    @pl.when(c == 1)
    def _():
        fill(others, mine, 0)

    hh[...], hlow[...] = split(hunit[...])
    places = ids[...]

    def step(i, carry):
        total, positive = carry
        here = pl.ds(pl.multiple_of(i * STEP, STEP), STEP)
        high, low = split(punit[here, :])
        ph[here, :] = high
        plow[here, :] = low
        scores = product(high, low, hh[...], hlow[...], ((1,), (1,))) * inv_temp
        e = jnp.exp(scores - inv_temp)
        expo[here, :] = e
        sums = jnp.sum(e, axis=1, keepdims=True)
        for k in range(STEP // 128):
            lanes = pl.ds(pl.multiple_of(i * STEP + k * 128, 128), 128)
            row_sums[:, lanes] = to_lanes(sums[k * 128 : (k + 1) * 128])
        match = wanted[here, :] == places
        total = total + jnp.sum(e.reshape(STEP // 8, 8, COLS), axis=0)
        positive = positive + jnp.sum(
            jnp.where(match, scores, 0.0).reshape(STEP // 8, 8, COLS), axis=0
        )
        return total, positive

    zero = jnp.zeros((8, COLS), jnp.float32)
    total, positive = lax.fori_loop(0, ROWS // STEP, step, (zero, zero))
    positive = jnp.sum(positive, axis=0, keepdims=True)
    row_sums[:, ROWS:] = sum(positive[:, k * 128 : (k + 1) * 128] for k in range(COLS // 128))
    total = jnp.sum(total, axis=0, keepdims=True)
    none, rest = jnp.zeros_like(total), jnp.zeros((1, SUMS - ROWS), jnp.float32)

    @pl.when(c == 0)
    def _():
        keep[...] = row_sums[...]
        send[...] = jnp.concatenate([total, none, rest], axis=1)

    @pl.when(c == 1)
    def _():
        keep[...] = jnp.concatenate([none, total, rest], axis=1)
        send[...] = row_sums[...]


def grads_kernel(place, ids, wanted, sums, other_sums, expo, ph, plow, hh, hlow, *refs):
    keeps, sends = refs[:2], refs[2:4]
    dh, dlow, pgrads, hgrads = refs[4:]
    x, y, c, zh, zl = (place[k] for k in range(5))
    first = c == 0
    scale = inv_temp / (2.0 * BATCH)
    rows = jnp.where(first, sums[...], other_sums[...])
    cols = jnp.where(first, other_sums[...], sums[...])
    row_term = jnp.sum(jnp.log(rows[:, :ROWS])) - 2.0 * jnp.sum(rows[:, ROWS:])
    col_term = jnp.sum(jnp.log(cols[:, : 2 * COLS]))
    row_inv = scale / rows[:, :ROWS]
    col_inv = scale / jnp.where(first, cols[:, :COLS], cols[:, COLS : 2 * COLS])
    places = ids[...]
    for i in range(ROWS // STEP):
        here = pl.ds(i * STEP, STEP)
        per_row = jnp.concatenate(
            [to_rows(row_inv[:, k : k + 128]) for k in range(i * STEP, (i + 1) * STEP, 128)], axis=0
        )
        match = wanted[here, :] == places
        d = expo[here, :] * (per_row + col_inv) - jnp.where(match, 2.0 * scale, 0.0)
        high, low = split(d)
        dh[here, :] = high
        dlow[here, :] = low
        pgrads[here, :] = product(high, low, hh[...], hlow[...], ((1,), (0,)))
    for k in range(COLS // 128):
        here = pl.ds(k * 128, 128)
        hgrads[here, :] = product(dh[:, here], dlow[:, here], ph[...], plow[...], ((0,), (0,)))

    def at(outs, j):
        line = (3, 1, 2, 0)[j]
        return outs[line // 2].at[line % 2]

    def packets(outs, term):
        for j, k, core, block in row_blocks(x, zl):
            at(outs, j)[k, core * B : (core + 1) * B, :] = block_at(pgrads, block)[...]
        for j in range(4):
            at(outs, j)[:, 2 * B :, :] = jnp.zeros((4, 8, D), jnp.float32) + term

    def headers(outs, term, other):
        for j, k, block in col_blocks(y, zh):
            at(outs, j)[k, other * B : (other + 1) * B, :] = block_at(hgrads, block)[...]
            at(outs, j)[k, (1 - other) * B : (2 - other) * B, :] = jnp.zeros((B, D), jnp.float32)
        for j in range(4):
            at(outs, j)[:, 2 * B :, :] = jnp.zeros((4, 8, D), jnp.float32) + term

    @pl.when(first)
    def _():
        packets(keeps, col_term)
        headers(sends, 0.0, 1)

    @pl.when(c == 1)
    def _():
        headers(keeps, row_term, 0)
        packets(sends, 0.0)


def in_vmem(count):
    return [pl.BlockSpec(memory_space=pltpu.VMEM)] * count


def call(kernel, operands, outs, scratch, flops):
    return pl.pallas_call(
        kernel,
        in_specs=[pl.BlockSpec(memory_space=pltpu.SMEM)] + in_vmem(len(operands) - 1),
        out_specs=in_vmem(len(outs)),
        out_shape=outs,
        scratch_shapes=scratch,
        compiler_params=pltpu.CompilerParams(vmem_limit_bytes=VMEM_LIMIT),
        cost_estimate=pl.CostEstimate(flops=flops, bytes_accessed=8 * 2**20, transcendentals=0),
    )(*operands)


def f32(*shape):
    return jax.ShapeDtypeStruct(shape, jnp.float32)


def b16(*shape):
    return jax.ShapeDtypeStruct(shape, jnp.bfloat16)


def unit_rows(values):
    norms = jnp.sqrt(jnp.sum(values * values, axis=1, keepdims=True) + eps_norm)
    return (values / norms, norms)


def unit_back(grads, units, norms):
    return (grads - units * jnp.sum(units * grads, axis=1, keepdims=True)) / norms


def together(*values):
    return lax.optimization_barrier(values)


def gather(first, packet, header):
    pair = jnp.concatenate(
        [
            jnp.where(first, packet, header),
            swap_core(jnp.where(first, header, packet)),
        ]
    )
    za = along_z(pair, 2, 1)
    zb = along_z(pair, 1, -1)
    line = jnp.stack([pair, za, zb, along_z(za, 1, 1)])
    ahead, behind = along_xy(line, 1), along_xy(line, -1)
    ahead, behind, line_again = together(ahead, behind, line)
    lines = [line, ahead, behind, along_xy(ahead, 1)]
    return lines, [swap_core(line) for line in lines]


def scatter(keeps, sends):
    far, ahead = (keeps[0] + swap_core(sends[0]))[:]
    behind, line = (keeps[1] + swap_core(sends[1]))[:]
    line = line + along_xy(ahead + along_xy(far, -1), -1) + along_xy(behind, 1)
    za = line[1] + along_z(line[3], 1, -1)
    return line[0] + along_z(za, 2, -1) + along_z(line[2], 1, 1)


def per_device(packet, header, partner):
    x, y, c, zh, zl = (lax.axis_index(name) for name in ALL)
    place = jnp.stack([x, y, c, zh, zl]).astype(jnp.int32)
    lane = np.arange(COLS)
    ids = lane // (NY * B) * (NL * NX * NY * NC * B) + lane // B % NY * (NC * B) + lane % B
    ids = jnp.asarray(ids, jnp.int32)[None, :]
    ids = ids + ((zl * NX + x) * (NY * NC * B) + c * B).astype(jnp.int32)
    wanted = lax.dynamic_slice(
        partner.reshape(NX, NY, NC, NH, NL, B), [0, y, 0, zh, 0, 0], (NX, 1, NC, 1, NL, B)
    ).reshape(ROWS, 1)

    first = c == 0
    lines, other_lines = gather(first, packet, header)
    flops = 2 * 3 * ROWS * COLS * D
    expo, ph, plow, hh, hlow, keep, send = call(
        scores_kernel,
        [place, ids, wanted] + lines + other_lines,
        [f32(ROWS, COLS), b16(ROWS, D), b16(ROWS, D), b16(COLS, D), b16(COLS, D)] + [f32(1, SUMS)] * 2,
        [pltpu.VMEM((ROWS, D), jnp.float32), pltpu.VMEM((COLS, D), jnp.float32), pltpu.VMEM((1, SUMS), jnp.float32)],
        flops,
    )
    sums = lax.all_to_all(
        jnp.broadcast_to((keep + swap_core(send))[None], (16, 1, SUMS)),
        ALL, 0, 0, axis_index_groups=groups(),
    )
    sums = jnp.sum(sums, axis=0)
    parts = call(
        grads_kernel,
        [place, ids, wanted, sums, swap_core(sums), expo, ph, plow, hh, hlow],
        [f32(2, 4, PAIR, D)] * 4,
        [
            pltpu.VMEM((ROWS, COLS), jnp.bfloat16),
            pltpu.VMEM((ROWS, COLS), jnp.bfloat16),
            pltpu.VMEM((ROWS, D), jnp.float32),
            pltpu.VMEM((COLS, D), jnp.float32),
        ],
        2 * flops,
    )
    pair = scatter(parts[:2], parts[2:])
    got = swap_core(pair[B:])
    own, other = pair[:B], got[:B]
    gpunit, ghunit = jnp.where(first, own, other), jnp.where(first, other, own)
    loss = inv_temp + (pair[2 * B, 0] + got[B, 0]) / (2.0 * BATCH)
    punit, pnorm = unit_rows(packet)
    hunit, hnorm = unit_rows(header)
    packet_grad = unit_back(gpunit, punit, pnorm)
    header_grad = unit_back(ghunit, hunit, hnorm)
    return (loss, packet_grad, header_grad)


def solution(mesh):
    mesh = Mesh(mesh.devices.reshape(NX, NY, NC, NH, NL), ALL)
    by_packet, by_header = P(ALL, None), P(("zh", "zl", "x", "y", "core"), None)
    return jax.shard_map(
        per_device,
        mesh=mesh,
        in_specs=(by_packet, by_header, P()),
        out_specs=(P(), by_packet, by_header),
        check_vma=False,
    )
```

```python
import functools

import jax
import jax.numpy as jnp
import numpy as np
from jax import lax
from jax.experimental import pallas as pl
from jax.experimental.pallas import tpu as pltpu
from jax.sharding import Mesh, PartitionSpec as P

inv_temp = 1.0 / 0.07
eps_norm = 1e-06
NX, NY, NC, NZ = 4, 4, 2, 16
NH, NL = 4, 4
ALL = ("x", "y", "core", "zh", "zl")
B = 40
D = 512
ROWS = NX * NC * NL * B
COLS = NY * NH * B
BATCH = NX * NY * NC * NZ * B
PAIR = 2 * B + 8
PLACES = (0, 1, -1, 2)
FLIPS = (0, 2, 1, 3)
VMEM_LIMIT = 48 * 2**20


def permute(value, source):
    pairs = []
    for x in range(NX):
        for y in range(NY):
            for c in range(NC):
                for z in range(NZ):
                    sx, sy, sc, sz = source(x, y, c, z)
                    src = (((sx % NX) * NY + sy % NY) * NC + sc) * NZ + sz
                    pairs.append((src, ((x * NY + y) * NC + c) * NZ + z))
    return lax.ppermute(value, ALL, pairs)


def along_xy(value, step):
    return permute(value, lambda x, y, c, z: (x + (1 - c) * step, y + c * step, c, z))


def along_z(value, flip, step):
    return permute(
        value, lambda x, y, c, z: (x, y, c, (z + NL * step) % NZ if c else z ^ flip)
    )


def swap_core(value):
    return permute(value, lambda x, y, c, z: (x, y, c ^ 1, z))


def groups():
    index = np.arange(NX * NY * NC * NZ).reshape(NX, NY, NC, NH, NL)
    found = []
    for i in range(4):
        for j in range(4):
            found.append(index[:, i, 0, j, :].reshape(-1).tolist())
            found.append(index[i, :, 1, :, j].reshape(-1).tolist())
    return found


def row_blocks(x, zl):
    found = []
    for j, dx in enumerate(PLACES):
        bx = lax.rem(x + dx + NX, NX)
        for k, flip in enumerate(FLIPS):
            for core in range(NC):
                found.append((j, k, core, (bx * NC + core) * NL + (zl ^ flip)))
    return found


def col_blocks(y, zh):
    found = []
    for j, dy in enumerate(PLACES):
        by = lax.rem(y + dy + NY, NY)
        for k, dz in enumerate(PLACES):
            found.append((j, k, lax.rem(zh + dz + NH, NH) * NY + by))
    return found


def block_at(ref, block):
    return ref.at[pl.ds(pl.multiple_of(block * B, 8), B), :]


def split(value):
    high = value.astype(jnp.bfloat16)
    return high, (value - high.astype(jnp.float32)).astype(jnp.bfloat16)


def product(a_high, a_low, b_high, b_low, dims):
    dot = functools.partial(
        lax.dot_general, dimension_numbers=(dims, ((), ())), preferred_element_type=jnp.float32
    )
    return dot(a_high, b_high) + (dot(a_high, b_low) + dot(a_low, b_high))


def eye():
    return lax.broadcasted_iota(jnp.int32, (128, 128), 0) == lax.broadcasted_iota(
        jnp.int32, (128, 128), 1
    )


def to_lanes(column):
    return jnp.sum(jnp.where(eye(), column, 0.0), axis=0, keepdims=True)


def to_rows(lanes):
    return jnp.sum(jnp.where(eye(), lanes, 0.0), axis=1, keepdims=True)


STEP = 256
SUMS = ROWS + 128
KEPT_F32 = 6 * ROWS
KEPT_B16 = 16 * ROWS


def kept(whole):
    starts = (0, ROWS, 2 * ROWS, 2 * ROWS + COLS)
    return [whole.at[pl.ds(start, n), :] for start, n in zip(starts, (ROWS, ROWS, COLS, COLS))]


def scores_kernel(place, ids, wanted, *refs):
    mine, others = refs[:4], refs[4:8]
    expo_out, halves_out, keep, send = refs[8:12]
    punit, hunit, row_sums, expo, ph, plow, hh, hlow, sems = refs[12:]
    ph_out, plow_out, hh_out, hlow_out = kept(halves_out)
    x, y, c, zh, zl = (place[k] for k in range(5))

    def unit(v):
        return v * (1.0 / jnp.sqrt(jnp.sum(v * v, axis=1, keepdims=True) + eps_norm))

    def fill(rows_in, cols_in, other):
        for j, k, block in col_blocks(y, zh):
            block_at(hunit, block)[...] = unit(cols_in[j][k, other * B : (other + 1) * B, :])
        for j, k, core, block in row_blocks(x, zl):
            block_at(punit, block)[...] = unit(rows_in[j][k, core * B : (core + 1) * B, :])

    @pl.when(c == 0)
    def _():
        fill(mine, others, 1)

    @pl.when(c == 1)
    def _():
        fill(others, mine, 0)

    hh[...], hlow[...] = split(hunit[...])
    whole = [
        pltpu.make_async_copy(hh, hh_out, sems.at[3]),
        pltpu.make_async_copy(hlow, hlow_out, sems.at[4]),
    ]
    for copy in whole:
        copy.start()
    places = ids[...]

    def copies(here):
        pairs = ((expo, expo_out), (ph, ph_out), (plow, plow_out))
        return [
            pltpu.make_async_copy(a.at[here, :], b.at[here, :], sems.at[k])
            for k, (a, b) in enumerate(pairs)
        ]

    total = positive = jnp.zeros((8, COLS), jnp.float32)
    for i in range(ROWS // STEP):
        here = pl.ds(i * STEP, STEP)
        high, low = split(punit[here, :])
        ph[here, :] = high
        plow[here, :] = low
        scores = product(high, low, hh[...], hlow[...], ((1,), (1,))) * inv_temp
        e = jnp.exp(scores - inv_temp)
        expo[here, :] = e
        if i:
            for copy in copies(pl.ds((i - 1) * STEP, STEP)):
                copy.wait()
        for copy in copies(here):
            copy.start()
        sums = jnp.sum(e, axis=1, keepdims=True)
        for k in range(0, STEP, 128):
            row_sums[:, pl.ds(i * STEP + k, 128)] = to_lanes(sums[k : k + 128])
        total = total + jnp.sum(e.reshape(STEP // 8, 8, COLS), axis=0)
        match = wanted[here, :] == places
        positive = positive + jnp.sum(
            jnp.where(match, scores, 0.0).reshape(STEP // 8, 8, COLS), axis=0
        )

    for copy in copies(pl.ds(ROWS - STEP, STEP)) + whole:
        copy.wait()
    positive = jnp.sum(positive, axis=0, keepdims=True)
    row_sums[:, ROWS:] = sum(positive[:, k * 128 : (k + 1) * 128] for k in range(COLS // 128))
    total = jnp.sum(total, axis=0, keepdims=True)
    none, rest = jnp.zeros_like(total), jnp.zeros((1, SUMS - ROWS), jnp.float32)

    @pl.when(c == 0)
    def _():
        keep[...] = row_sums[...]
        send[...] = jnp.concatenate([total, none, rest], axis=1)

    @pl.when(c == 1)
    def _():
        keep[...] = jnp.concatenate([none, total, rest], axis=1)
        send[...] = row_sums[...]


def grads_kernel(place, ids, wanted, sums, other_sums, expo_in, halves_in, *refs):
    keeps, sends = refs[:2], refs[2:4]
    dh, dlow, pgrads, hgrads, expo, ph, plow, hh, hlow, sems = refs[4:]
    ph_in, plow_in, hh_in, hlow_in = kept(halves_in)
    steps = [pl.ds(i * STEP, STEP) for i in range(ROWS // STEP)]
    whole = [
        pltpu.make_async_copy(a, b, sems.at[k])
        for k, (a, b) in enumerate(((hh_in, hh), (hlow_in, hlow), (ph_in, ph), (plow_in, plow)))
    ]
    chunks = [
        pltpu.make_async_copy(expo_in.at[here, :], expo.at[here, :], sems.at[4 + i])
        for i, here in enumerate(steps)
    ]
    for copy in whole[:2] + chunks + whole[2:]:
        copy.start()
    x, y, c, zh, zl = (place[k] for k in range(5))
    first = c == 0
    scale = inv_temp / (2.0 * BATCH)
    rows = jnp.where(first, sums[...], other_sums[...])
    cols = jnp.where(first, other_sums[...], sums[...])
    row_term = jnp.sum(jnp.log(rows[:, :ROWS])) - 2.0 * jnp.sum(rows[:, ROWS:])
    col_term = jnp.sum(jnp.log(cols[:, : 2 * COLS]))
    row_inv = scale / rows[:, :ROWS]
    col_inv = scale / jnp.where(first, cols[:, :COLS], cols[:, COLS : 2 * COLS])
    places = ids[...]
    for copy in whole[:2]:
        copy.wait()
    for i, here in enumerate(steps):
        chunks[i].wait()
        per_row = jnp.concatenate(
            [to_rows(row_inv[:, k : k + 128]) for k in range(i * STEP, (i + 1) * STEP, 128)], axis=0
        )
        match = wanted[here, :] == places
        d = expo[here, :] * (per_row + col_inv) - jnp.where(match, 2.0 * scale, 0.0)
        high, low = split(d)
        dh[here, :] = high
        dlow[here, :] = low
        pgrads[here, :] = product(high, low, hh[...], hlow[...], ((1,), (0,)))
    for copy in whole[2:]:
        copy.wait()
    for k in range(COLS // 128):
        here = pl.ds(k * 128, 128)
        hgrads[here, :] = product(dh[:, here], dlow[:, here], ph[...], plow[...], ((0,), (0,)))

    def at(outs, j):
        line = (3, 1, 2, 0)[j]
        return outs[line // 2].at[line % 2]

    def packets(outs, term):
        for j, k, core, block in row_blocks(x, zl):
            at(outs, j)[k, core * B : (core + 1) * B, :] = block_at(pgrads, block)[...]
        for j in range(4):
            at(outs, j)[:, 2 * B :, :] = jnp.zeros((4, 8, D), jnp.float32) + term

    def headers(outs, term, other):
        for j, k, block in col_blocks(y, zh):
            at(outs, j)[k, other * B : (other + 1) * B, :] = block_at(hgrads, block)[...]
            at(outs, j)[k, (1 - other) * B : (2 - other) * B, :] = jnp.zeros((B, D), jnp.float32)
        for j in range(4):
            at(outs, j)[:, 2 * B :, :] = jnp.zeros((4, 8, D), jnp.float32) + term

    @pl.when(first)
    def _():
        packets(keeps, col_term)
        headers(sends, 0.0, 1)

    @pl.when(c == 1)
    def _():
        headers(keeps, row_term, 0)
        packets(sends, 0.0)


def last_kernel(place, packet, header, pair, got, packet_grad, header_grad, loss):
    first = place[2] == 0
    own, other = pair[:B, :], got[:B, :]

    def back(values, grads):
        norms = jnp.sqrt(jnp.sum(values * values, axis=1, keepdims=True) + eps_norm)
        inverse = 1.0 / norms
        units = values * inverse
        return (grads - units * jnp.sum(units * grads, axis=1, keepdims=True)) * inverse

    packet_grad[...] = back(packet[...], jnp.where(first, own, other))
    header_grad[...] = back(header[...], jnp.where(first, other, own))
    term = jnp.max(pair[2 * B :, :128] + got[B:, :128])
    loss[0, 0] = inv_temp + term / (2.0 * BATCH)


IN_VMEM = pl.BlockSpec(memory_space=pltpu.VMEM)
IN_SMEM = pl.BlockSpec(memory_space=pltpu.SMEM)
IN_PLACE = pl.BlockSpec(memory_space=pl.ANY)


def call(kernel, operands, in_specs, outs, out_specs, scratch, flops):
    return pl.pallas_call(
        kernel,
        in_specs=[IN_SMEM] + in_specs,
        out_specs=out_specs,
        out_shape=outs,
        scratch_shapes=scratch,
        compiler_params=pltpu.CompilerParams(vmem_limit_bytes=VMEM_LIMIT),
        cost_estimate=pl.CostEstimate(flops=flops, bytes_accessed=8 * 2**20, transcendentals=0),
    )(*operands)


def f32(*shape):
    return jax.ShapeDtypeStruct(shape, jnp.float32)


def b16(*shape):
    return jax.ShapeDtypeStruct(shape, jnp.bfloat16)


def together(*values):
    return lax.optimization_barrier(values)


def gather(first, packet, header):
    pair = jnp.concatenate(
        [
            jnp.where(first, packet, header),
            swap_core(jnp.where(first, header, packet)),
        ]
    )
    za = along_z(pair, 2, 1)
    zb = along_z(pair, 1, -1)
    line = jnp.stack([pair, za, zb, along_z(za, 1, 1)])
    ahead, behind = along_xy(line, 1), along_xy(line, -1)
    lines = [line, ahead, behind, along_xy(ahead, 1)]
    return lines, [swap_core(line) for line in lines]


def scatter(keeps, sends):
    far, ahead = (keeps[0] + swap_core(sends[0]))[:]
    behind, line = (keeps[1] + swap_core(sends[1]))[:]
    line = line + along_xy(ahead, -1) + along_xy(behind + along_xy(far, 1), 1)
    zb = line[2] + along_z(line[3], 2, 1)
    return line[0] + along_z(line[1], 2, -1) + along_z(zb, 1, 1)


def per_device(packet, header, partner):
    x, y, c, zh, zl = (lax.axis_index(name) for name in ALL)
    place = jnp.stack([x, y, c, zh, zl]).astype(jnp.int32)
    lane = np.arange(COLS)
    ids = lane // (NY * B) * (NL * NX * NY * NC * B) + lane // B % NY * (NC * B) + lane % B
    ids = jnp.asarray(ids, jnp.int32)[None, :]
    ids = ids + ((zl * NX + x) * (NY * NC * B) + c * B).astype(jnp.int32)
    wanted = lax.dynamic_slice(
        partner.reshape(NX, NY, NC, NH, NL, B), [0, y, 0, zh, 0, 0], (NX, 1, NC, 1, NL, B)
    ).reshape(ROWS, 1)

    first = c == 0
    lines, other_lines = gather(first, packet, header)
    flops = 2 * 3 * ROWS * COLS * D
    tiles = [((ROWS, COLS), jnp.float32)] + [((ROWS, D), jnp.bfloat16)] * 2
    tiles += [((COLS, D), jnp.bfloat16)] * 2
    held = [pltpu.VMEM(*tile) for tile in tiles]
    expo, halves, keep, send = call(
        scores_kernel,
        [place, ids, wanted] + lines + other_lines,
        [IN_VMEM] * 10,
        [f32(KEPT_F32, COLS), b16(KEPT_B16, D), f32(1, SUMS), f32(1, SUMS)],
        [IN_PLACE] * 2 + [IN_VMEM] * 2,
        [pltpu.VMEM((ROWS, D), jnp.float32), pltpu.VMEM((COLS, D), jnp.float32), pltpu.VMEM((1, SUMS), jnp.float32)]
        + held
        + [pltpu.SemaphoreType.DMA((5,))],
        flops,
    )
    sums = lax.all_to_all(
        jnp.broadcast_to((keep + swap_core(send))[None], (16, 1, SUMS)),
        ALL, 0, 0, axis_index_groups=groups(),
    )
    sums = jnp.sum(sums, axis=0)
    parts = call(
        grads_kernel,
        [place, ids, wanted, sums, swap_core(sums), expo, halves],
        [IN_VMEM] * 4 + [IN_PLACE] * 2,
        [f32(2, 4, PAIR, D)] * 4,
        [IN_VMEM] * 4,
        [
            pltpu.VMEM((ROWS, COLS), jnp.bfloat16),
            pltpu.VMEM((ROWS, COLS), jnp.bfloat16),
            pltpu.VMEM((ROWS, D), jnp.float32),
            pltpu.VMEM((COLS, D), jnp.float32),
        ]
        + held
        + [pltpu.SemaphoreType.DMA((4 + ROWS // STEP,))],
        2 * flops,
    )
    pair = scatter(parts[:2], parts[2:])
    packet_grad, header_grad, loss = call(
        last_kernel,
        [place, packet, header, pair, swap_core(pair[B:])],
        [IN_VMEM] * 4,
        [f32(B, D), f32(B, D), f32(1, 1)],
        [IN_VMEM, IN_VMEM, IN_SMEM],
        [],
        10 * B * D,
    )
    return (loss[0, 0], packet_grad, header_grad)


def solution(mesh):
    mesh = Mesh(mesh.devices.reshape(NX, NY, NC, NH, NL), ALL)
    by_packet, by_header = P(ALL, None), P(("zh", "zl", "x", "y", "core"), None)
    return jax.shard_map(
        per_device,
        mesh=mesh,
        in_specs=(by_packet, by_header, P()),
        out_specs=(P(), by_packet, by_header),
        check_vma=False,
    )
```

```python
import functools

import jax
import jax.numpy as jnp
import numpy as np
from jax import lax
from jax.experimental import pallas as pl
from jax.experimental.pallas import tpu as pltpu
from jax.sharding import Mesh, PartitionSpec as P

inv_temp = 1.0 / 0.07
eps_norm = 1e-06
NX, NY, NC, NZ = 4, 4, 2, 16
NH, NL = 4, 4
ALL = ("x", "y", "core", "zh", "zl")
B = 40
D = 512
ROWS = NX * NC * NL * B
COLS = NY * NH * B
BATCH = NX * NY * NC * NZ * B
PAIR = 2 * B + 8
PLACES = (0, 1, -1, 2)
FLIPS = (0, 2, 1, 3)
VMEM_LIMIT = 48 * 2**20


def permute(value, source):
    pairs = []
    for x in range(NX):
        for y in range(NY):
            for c in range(NC):
                for z in range(NZ):
                    sx, sy, sc, sz = source(x, y, c, z)
                    src = (((sx % NX) * NY + sy % NY) * NC + sc) * NZ + sz
                    pairs.append((src, ((x * NY + y) * NC + c) * NZ + z))
    return lax.ppermute(value, ALL, pairs)


def along_xy(value, step):
    return permute(value, lambda x, y, c, z: (x + (1 - c) * step, y + c * step, c, z))


def along_z(value, flip, step):
    return permute(
        value,
        lambda x, y, c, z: (x, y, c, (z + NL * step * (1 - 2 * (z % 2))) % NZ if c else z ^ flip),
    )


def swap_core(value):
    return permute(value, lambda x, y, c, z: (x, y, c ^ 1, z))


def groups():
    index = np.arange(NX * NY * NC * NZ).reshape(NX, NY, NC, NH, NL)
    found = []
    for i in range(4):
        for j in range(4):
            found.append(index[:, i, 0, j, :].reshape(-1).tolist())
            found.append(index[i, :, 1, :, j].reshape(-1).tolist())
    return found


def row_blocks(x, zl):
    found = []
    for j, dx in enumerate(PLACES):
        bx = lax.rem(x + dx + NX, NX)
        for k, flip in enumerate(FLIPS):
            for core in range(NC):
                found.append((j, k, core, (bx * NC + core) * NL + (zl ^ flip)))
    return found


def col_blocks(y, zh, zl):
    found = []
    s = 1 - 2 * lax.rem(zl, 2)
    for j, dy in enumerate(PLACES):
        by = lax.rem(y + dy + NY, NY)
        for k, dz in enumerate(PLACES):
            found.append((j, k, lax.rem(zh + s * dz + NH, NH) * NY + by))
    return found


def block_at(ref, block):
    return ref.at[pl.ds(pl.multiple_of(block * B, 8), B), :]


def split(value):
    high = value.astype(jnp.bfloat16)
    return high, (value - high.astype(jnp.float32)).astype(jnp.bfloat16)


def product(a_high, a_low, b_high, b_low, dims):
    dot = functools.partial(
        lax.dot_general, dimension_numbers=(dims, ((), ())), preferred_element_type=jnp.float32
    )
    return dot(a_high, b_high) + (dot(a_high, b_low) + dot(a_low, b_high))


def wide_product(high, low, both, axis):
    dot = functools.partial(
        lax.dot_general,
        dimension_numbers=(((axis,), (0,)), ((), ())),
        preferred_element_type=jnp.float32,
    )
    wide = dot(high, both[...])
    return wide[:, :D] + (wide[:, D:] + dot(low, both[:, :D]))


def eye():
    return lax.broadcasted_iota(jnp.int32, (128, 128), 0) == lax.broadcasted_iota(
        jnp.int32, (128, 128), 1
    )


def to_lanes(column):
    return jnp.sum(jnp.where(eye(), column, 0.0), axis=0, keepdims=True)


def to_rows(lanes):
    return jnp.sum(jnp.where(eye(), lanes, 0.0), axis=1, keepdims=True)


STEP = 256
SUMS = ROWS + 128
KEPT_F32 = 6 * ROWS
KEPT_B16 = 16 * ROWS


def kept(whole):
    starts = (0, ROWS, 2 * ROWS, 2 * ROWS + COLS)
    return [whole.at[pl.ds(start, n), :] for start, n in zip(starts, (ROWS, ROWS, COLS, COLS))]


def scores_kernel(place, ids, wanted, *refs):
    mine, others = refs[:4], refs[4:8]
    expo_out, halves_out, keep, send = refs[8:12]
    punit, hunit, row_sums, expo, ph, plow, hh, hlow, sems = refs[12:]
    ph_out, plow_out, hh_out, hlow_out = kept(halves_out)
    x, y, c, zh, zl = (place[k] for k in range(5))

    def unit(v):
        return v * (1.0 / jnp.sqrt(jnp.sum(v * v, axis=1, keepdims=True) + eps_norm))

    def fill(rows_in, cols_in, other):
        for j, k, block in col_blocks(y, zh, zl):
            block_at(hunit, block)[...] = unit(cols_in[j][k, other * B : (other + 1) * B, :])
        for j, k, core, block in row_blocks(x, zl):
            block_at(punit, block)[...] = unit(rows_in[j][k, core * B : (core + 1) * B, :])

    @pl.when(c == 0)
    def _():
        fill(mine, others, 1)

    @pl.when(c == 1)
    def _():
        fill(others, mine, 0)

    hh[...], hlow[...] = split(hunit[...])
    whole = [
        pltpu.make_async_copy(hh, hh_out, sems.at[3]),
        pltpu.make_async_copy(hlow, hlow_out, sems.at[4]),
    ]
    for copy in whole:
        copy.start()
    places = ids[...]

    def copies(here):
        pairs = ((expo, expo_out), (ph, ph_out), (plow, plow_out))
        return [
            pltpu.make_async_copy(a.at[here, :], b.at[here, :], sems.at[k])
            for k, (a, b) in enumerate(pairs)
        ]

    total = positive = jnp.zeros((8, COLS), jnp.float32)
    for i in range(ROWS // STEP):
        here = pl.ds(i * STEP, STEP)
        high, low = split(punit[here, :])
        ph[here, :] = high
        plow[here, :] = low
        scores = product(high, low, hh[...], hlow[...], ((1,), (1,))) * inv_temp
        e = jnp.exp(scores - inv_temp)
        expo[here, :] = e
        if i:
            for copy in copies(pl.ds((i - 1) * STEP, STEP)):
                copy.wait()
        for copy in copies(here):
            copy.start()
        sums = jnp.sum(e, axis=1, keepdims=True)
        for k in range(0, STEP, 128):
            row_sums[:, pl.ds(i * STEP + k, 128)] = to_lanes(sums[k : k + 128])
        total = total + jnp.sum(e.reshape(STEP // 8, 8, COLS), axis=0)
        match = wanted[here, :] == places
        positive = positive + jnp.sum(
            jnp.where(match, scores, 0.0).reshape(STEP // 8, 8, COLS), axis=0
        )

    for copy in copies(pl.ds(ROWS - STEP, STEP)) + whole:
        copy.wait()
    positive = jnp.sum(positive, axis=0, keepdims=True)
    row_sums[:, ROWS:] = sum(positive[:, k * 128 : (k + 1) * 128] for k in range(COLS // 128))
    total = jnp.sum(total, axis=0, keepdims=True)
    none, rest = jnp.zeros_like(total), jnp.zeros((1, SUMS - ROWS), jnp.float32)

    @pl.when(c == 0)
    def _():
        keep[...] = row_sums[...]
        send[...] = jnp.concatenate([total, none, rest], axis=1)

    @pl.when(c == 1)
    def _():
        keep[...] = jnp.concatenate([none, total, rest], axis=1)
        send[...] = row_sums[...]


def grads_kernel(place, ids, wanted, sums, other_sums, expo_in, halves_in, *refs):
    keeps, sends = refs[:2], refs[2:4]
    dh, dlow, pgrads, hgrads, expo, pboth, hboth, sems = refs[4:]
    high_half, low_half = pl.ds(0, D), pl.ds(D, D)
    hh, hlow = hboth.at[:, high_half], hboth.at[:, low_half]
    ph, plow = pboth.at[:, high_half], pboth.at[:, low_half]
    ph_in, plow_in, hh_in, hlow_in = kept(halves_in)
    steps = [pl.ds(i * STEP, STEP) for i in range(ROWS // STEP)]
    whole = [
        pltpu.make_async_copy(a, b, sems.at[k])
        for k, (a, b) in enumerate(((hh_in, hh), (hlow_in, hlow), (ph_in, ph), (plow_in, plow)))
    ]
    chunks = [
        pltpu.make_async_copy(expo_in.at[here, :], expo.at[here, :], sems.at[4 + i])
        for i, here in enumerate(steps)
    ]
    for copy in whole[:2] + chunks + whole[2:]:
        copy.start()
    x, y, c, zh, zl = (place[k] for k in range(5))
    first = c == 0
    scale = inv_temp / (2.0 * BATCH)
    rows = jnp.where(first, sums[...], other_sums[...])
    cols = jnp.where(first, other_sums[...], sums[...])
    row_term = jnp.sum(jnp.log(rows[:, :ROWS])) - 2.0 * jnp.sum(rows[:, ROWS:])
    col_term = jnp.sum(jnp.log(cols[:, : 2 * COLS]))
    row_inv = scale / rows[:, :ROWS]
    col_inv = scale / jnp.where(first, cols[:, :COLS], cols[:, COLS : 2 * COLS])
    places = ids[...]
    for copy in whole[:2]:
        copy.wait()
    for i, here in enumerate(steps):
        chunks[i].wait()
        per_row = jnp.concatenate(
            [to_rows(row_inv[:, k : k + 128]) for k in range(i * STEP, (i + 1) * STEP, 128)], axis=0
        )
        match = wanted[here, :] == places
        d = expo[here, :] * (per_row + col_inv) - jnp.where(match, 2.0 * scale, 0.0)
        high, low = split(d)
        dh[here, :] = high
        dlow[here, :] = low
        pgrads[here, :] = wide_product(high, low, hboth, 1)
    for copy in whole[2:]:
        copy.wait()
    for k in range(COLS // 128):
        here = pl.ds(k * 128, 128)
        hgrads[here, :] = wide_product(dh[:, here], dlow[:, here], pboth, 0)

    def at(outs, j):
        line = (3, 1, 2, 0)[j]
        return outs[line // 2].at[line % 2]

    def packets(outs, term):
        for j, k, core, block in row_blocks(x, zl):
            at(outs, j)[k, core * B : (core + 1) * B, :] = block_at(pgrads, block)[...]
        for j in range(4):
            at(outs, j)[:, 2 * B :, :] = jnp.zeros((4, 8, D), jnp.float32) + term

    def headers(outs, term, other):
        for j, k, block in col_blocks(y, zh, zl):
            at(outs, j)[k, other * B : (other + 1) * B, :] = block_at(hgrads, block)[...]
            at(outs, j)[k, (1 - other) * B : (2 - other) * B, :] = jnp.zeros((B, D), jnp.float32)
        for j in range(4):
            at(outs, j)[:, 2 * B :, :] = jnp.zeros((4, 8, D), jnp.float32) + term

    @pl.when(first)
    def _():
        packets(keeps, col_term)
        headers(sends, 0.0, 1)

    @pl.when(c == 1)
    def _():
        headers(keeps, row_term, 0)
        packets(sends, 0.0)


def last_kernel(place, packet, header, pair, got, packet_grad, header_grad, loss):
    first = place[2] == 0
    own, other = pair[:B, :], got[:B, :]

    def back(values, grads):
        norms = jnp.sqrt(jnp.sum(values * values, axis=1, keepdims=True) + eps_norm)
        inverse = 1.0 / norms
        units = values * inverse
        return (grads - units * jnp.sum(units * grads, axis=1, keepdims=True)) * inverse

    packet_grad[...] = back(packet[...], jnp.where(first, own, other))
    header_grad[...] = back(header[...], jnp.where(first, other, own))
    term = jnp.max(pair[2 * B :, :128] + got[B:, :128])
    loss[0, 0] = inv_temp + term / (2.0 * BATCH)


IN_VMEM = pl.BlockSpec(memory_space=pltpu.VMEM)
IN_SMEM = pl.BlockSpec(memory_space=pltpu.SMEM)
IN_PLACE = pl.BlockSpec(memory_space=pl.ANY)


def call(kernel, operands, in_specs, outs, out_specs, scratch, flops):
    return pl.pallas_call(
        kernel,
        in_specs=[IN_SMEM] + in_specs,
        out_specs=out_specs,
        out_shape=outs,
        scratch_shapes=scratch,
        compiler_params=pltpu.CompilerParams(vmem_limit_bytes=VMEM_LIMIT),
        cost_estimate=pl.CostEstimate(flops=flops, bytes_accessed=8 * 2**20, transcendentals=0),
    )(*operands)


def f32(*shape):
    return jax.ShapeDtypeStruct(shape, jnp.float32)


def b16(*shape):
    return jax.ShapeDtypeStruct(shape, jnp.bfloat16)


def together(*values):
    return lax.optimization_barrier(values)


def gather(first, packet, header):
    pair = jnp.concatenate(
        [
            jnp.where(first, packet, header),
            swap_core(jnp.where(first, header, packet)),
        ]
    )
    za = along_z(pair, 2, 1)
    zb = along_z(pair, 1, -1)
    line = jnp.stack([pair, za, zb, along_z(za, 1, 1)])
    ahead, behind = along_xy(line, 1), along_xy(line, -1)
    lines = [line, ahead, behind, along_xy(ahead, 1)]
    return lines, [swap_core(line) for line in lines]


def scatter(keeps, sends):
    far, ahead = (keeps[0] + swap_core(sends[0]))[:]
    behind, line = (keeps[1] + swap_core(sends[1]))[:]
    line = line + along_xy(ahead, -1) + along_xy(behind + along_xy(far, 1), 1)
    za = line[1] + along_z(line[3], 1, -1)
    return line[0] + along_z(za, 2, -1) + along_z(line[2], 1, 1)


def per_device(packet, header, partner):
    x, y, c, zh, zl = (lax.axis_index(name) for name in ALL)
    place = jnp.stack([x, y, c, zh, zl]).astype(jnp.int32)
    lane = np.arange(COLS)
    ids = lane // (NY * B) * (NL * NX * NY * NC * B) + lane // B % NY * (NC * B) + lane % B
    ids = jnp.asarray(ids, jnp.int32)[None, :]
    ids = ids + ((zl * NX + x) * (NY * NC * B) + c * B).astype(jnp.int32)
    wanted = lax.dynamic_slice(
        partner.reshape(NX, NY, NC, NH, NL, B), [0, y, 0, zh, 0, 0], (NX, 1, NC, 1, NL, B)
    ).reshape(ROWS, 1)

    first = c == 0
    lines, other_lines = gather(first, packet, header)
    flops = 2 * 3 * ROWS * COLS * D
    tiles = [((ROWS, COLS), jnp.float32)] + [((ROWS, D), jnp.bfloat16)] * 2
    tiles += [((COLS, D), jnp.bfloat16)] * 2
    held = [pltpu.VMEM(*tile) for tile in tiles]
    expo, halves, keep, send = call(
        scores_kernel,
        [place, ids, wanted] + lines + other_lines,
        [IN_VMEM] * 10,
        [f32(KEPT_F32, COLS), b16(KEPT_B16, D), f32(1, SUMS), f32(1, SUMS)],
        [IN_PLACE] * 2 + [IN_VMEM] * 2,
        [pltpu.VMEM((ROWS, D), jnp.float32), pltpu.VMEM((COLS, D), jnp.float32), pltpu.VMEM((1, SUMS), jnp.float32)]
        + held
        + [pltpu.SemaphoreType.DMA((5,))],
        flops,
    )
    sums = lax.all_to_all(
        jnp.broadcast_to((keep + swap_core(send))[None], (16, 1, SUMS)),
        ALL, 0, 0, axis_index_groups=groups(),
    )
    sums = jnp.sum(sums, axis=0)
    parts = call(
        grads_kernel,
        [place, ids, wanted, sums, swap_core(sums), expo, halves],
        [IN_VMEM] * 4 + [IN_PLACE] * 2,
        [f32(2, 4, PAIR, D)] * 4,
        [IN_VMEM] * 4,
        [
            pltpu.VMEM((ROWS, COLS), jnp.bfloat16),
            pltpu.VMEM((ROWS, COLS), jnp.bfloat16),
            pltpu.VMEM((ROWS, D), jnp.float32),
            pltpu.VMEM((COLS, D), jnp.float32),
            pltpu.VMEM((ROWS, COLS), jnp.float32),
            pltpu.VMEM((ROWS, 2 * D), jnp.bfloat16),
            pltpu.VMEM((COLS, 2 * D), jnp.bfloat16),
            pltpu.SemaphoreType.DMA((4 + ROWS // STEP,)),
        ],
        2 * flops,
    )
    pair = scatter(parts[:2], parts[2:])
    packet_grad, header_grad, loss = call(
        last_kernel,
        [place, packet, header, pair, swap_core(pair[B:])],
        [IN_VMEM] * 4,
        [f32(B, D), f32(B, D), f32(1, 1)],
        [IN_VMEM, IN_VMEM, IN_SMEM],
        [],
        10 * B * D,
    )
    return (loss[0, 0], packet_grad, header_grad)


def solution(mesh):
    mesh = Mesh(mesh.devices.reshape(NX, NY, NC, NH, NL), ALL)
    by_packet, by_header = P(ALL, None), P(("zh", "zl", "x", "y", "core"), None)
    return jax.shard_map(
        per_device,
        mesh=mesh,
        in_specs=(by_packet, by_header, P()),
        out_specs=(P(), by_packet, by_header),
        check_vma=False,
    )
```

```python
import functools
import math

import jax
import jax.numpy as jnp
import numpy as np
from jax import lax
from jax.experimental import pallas as pl
from jax.experimental.pallas import tpu as pltpu
from jax.sharding import Mesh, PartitionSpec as P

inv_temp = 1.0 / 0.07
eps_norm = 1e-06
LOG2_SCALE = inv_temp * math.log2(math.e)
NX, NY, NC, NZ = 4, 4, 2, 16
NH, NL = 4, 4
ALL = ("x", "y", "core", "zh", "zl")
B = 40
D = 512
ROWS = NX * NC * NL * B
COLS = NY * NH * B
BATCH = NX * NY * NC * NZ * B
PAIR = 2 * B + 8
PLACES = (0, 1, -1, 2)
FLIPS = (0, 2, 1, 3)
VMEM_LIMIT = 48 * 2**20


def permute(value, source):
    pairs = []
    for x in range(NX):
        for y in range(NY):
            for c in range(NC):
                for z in range(NZ):
                    sx, sy, sc, sz = source(x, y, c, z)
                    src = (((sx % NX) * NY + sy % NY) * NC + sc) * NZ + sz
                    pairs.append((src, ((x * NY + y) * NC + c) * NZ + z))
    return lax.ppermute(value, ALL, pairs)


def along_xy(value, step):
    return permute(value, lambda x, y, c, z: (x + (1 - c) * step, y + c * step, c, z))


def along_z(value, flip, step):
    return permute(
        value,
        lambda x, y, c, z: (x, y, c, (z + NL * step * (1 - 2 * (z % 2))) % NZ if c else z ^ flip),
    )


def swap_core(value):
    return permute(value, lambda x, y, c, z: (x, y, c ^ 1, z))


def groups():
    index = np.arange(NX * NY * NC * NZ).reshape(NX, NY, NC, NH, NL)
    found = []
    for i in range(4):
        for j in range(4):
            found.append(index[:, i, 0, j, :].reshape(-1).tolist())
            found.append(index[i, :, 1, :, j].reshape(-1).tolist())
    return found


def row_blocks(x, zl):
    found = []
    for j, dx in enumerate(PLACES):
        bx = lax.rem(x + dx + NX, NX)
        for k, flip in enumerate(FLIPS):
            for core in range(NC):
                found.append((j, k, core, (bx * NC + core) * NL + (zl ^ flip)))
    return found


def col_blocks(y, zh, zl):
    found = []
    s = 1 - 2 * lax.rem(zl, 2)
    for j, dy in enumerate(PLACES):
        by = lax.rem(y + dy + NY, NY)
        for k, dz in enumerate(PLACES):
            found.append((j, k, lax.rem(zh + s * dz + NH, NH) * NY + by))
    return found


def block_at(ref, block):
    return ref.at[pl.ds(pl.multiple_of(block * B, 8), B), :]


def split(value):
    high = value.astype(jnp.bfloat16)
    return high, (value - high.astype(jnp.float32)).astype(jnp.bfloat16)


def product(a_high, a_low, b_high, b_low, dims):
    dot = functools.partial(
        lax.dot_general, dimension_numbers=(dims, ((), ())), preferred_element_type=jnp.float32
    )
    return dot(a_high, b_high) + (dot(a_high, b_low) + dot(a_low, b_high))


def wide_product(high, low, both, axis):
    dot = functools.partial(
        lax.dot_general,
        dimension_numbers=(((axis,), (0,)), ((), ())),
        preferred_element_type=jnp.float32,
    )
    wide = dot(high, both[...])
    return wide[:, :D] + (wide[:, D:] + dot(low, both[:, :D]))


def eye():
    return lax.broadcasted_iota(jnp.int32, (128, 128), 0) == lax.broadcasted_iota(
        jnp.int32, (128, 128), 1
    )


def to_lanes(column):
    return jnp.sum(jnp.where(eye(), column, 0.0), axis=0, keepdims=True)


def to_rows(lanes):
    return jnp.sum(jnp.where(eye(), lanes, 0.0), axis=1, keepdims=True)


STEP = 256
SUMS = ROWS + 128
KEPT_F32 = 6 * ROWS
KEPT_B16 = 16 * ROWS


def kept(whole):
    starts = (0, ROWS, 2 * ROWS, 2 * ROWS + COLS)
    return [whole.at[pl.ds(start, n), :] for start, n in zip(starts, (ROWS, ROWS, COLS, COLS))]


def scores_kernel(place, ids, wanted, *refs):
    mine, others = refs[:4], refs[4:8]
    expo_out, halves_out, keep, send = refs[8:12]
    punit, hunit, row_sums, expo, ph, plow, hh, hlow, sems = refs[12:]
    ph_out, plow_out, hh_out, hlow_out = kept(halves_out)
    x, y, c, zh, zl = (place[k] for k in range(5))

    def unit(v):
        return v * (1.0 / jnp.sqrt(jnp.sum(v * v, axis=1, keepdims=True) + eps_norm))

    def fill(rows_in, cols_in, other):
        for j, k, block in col_blocks(y, zh, zl):
            block_at(hunit, block)[...] = unit(cols_in[j][k, other * B : (other + 1) * B, :])
        for j, k, core, block in row_blocks(x, zl):
            block_at(punit, block)[...] = unit(rows_in[j][k, core * B : (core + 1) * B, :])

    @pl.when(c == 0)
    def _():
        fill(mine, others, 1)

    @pl.when(c == 1)
    def _():
        fill(others, mine, 0)

    hh[...], hlow[...] = split(hunit[...])
    turned_high, turned_low = split(hunit[...].T)
    whole = [
        pltpu.make_async_copy(hh, hh_out, sems.at[3]),
        pltpu.make_async_copy(hlow, hlow_out, sems.at[4]),
    ]
    for copy in whole:
        copy.start()
    places = ids[...]

    def copies(here):
        pairs = ((expo, expo_out), (ph, ph_out), (plow, plow_out))
        return [
            pltpu.make_async_copy(a.at[here, :], b.at[here, :], sems.at[k])
            for k, (a, b) in enumerate(pairs)
        ]

    total = positive = jnp.zeros((8, COLS), jnp.float32)
    for i in range(ROWS // STEP):
        here = pl.ds(i * STEP, STEP)
        high, low = split(punit[here, :])
        ph[here, :] = high
        plow[here, :] = low
        cosines = product(high, low, turned_high, turned_low, ((1,), (0,)))
        e = jnp.exp2(cosines * LOG2_SCALE - LOG2_SCALE)
        expo[here, :] = e
        if i:
            for copy in copies(pl.ds((i - 1) * STEP, STEP)):
                copy.wait()
        for copy in copies(here):
            copy.start()
        sums = jnp.sum(e, axis=1, keepdims=True)
        for k in range(0, STEP, 128):
            row_sums[:, pl.ds(i * STEP + k, 128)] = to_lanes(sums[k : k + 128])
        total = total + jnp.sum(e.reshape(STEP // 8, 8, COLS), axis=0)
        match = wanted[here, :] == places
        positive = positive + jnp.sum(
            jnp.where(match, cosines, 0.0).reshape(STEP // 8, 8, COLS), axis=0
        )

    for copy in copies(pl.ds(ROWS - STEP, STEP)) + whole:
        copy.wait()
    positive = jnp.sum(positive, axis=0, keepdims=True)
    row_sums[:, ROWS:] = inv_temp * sum(
        positive[:, k * 128 : (k + 1) * 128] for k in range(COLS // 128)
    )
    total = jnp.sum(total, axis=0, keepdims=True)
    none, rest = jnp.zeros_like(total), jnp.zeros((1, SUMS - ROWS), jnp.float32)

    @pl.when(c == 0)
    def _():
        keep[...] = row_sums[...]
        send[...] = jnp.concatenate([total, none, rest], axis=1)

    @pl.when(c == 1)
    def _():
        keep[...] = jnp.concatenate([none, total, rest], axis=1)
        send[...] = row_sums[...]


def grads_kernel(place, ids, wanted, sums, other_sums, expo_in, halves_in, *refs):
    keeps, sends = refs[:2], refs[2:4]
    dh, dlow, pgrads, hgrads, expo, pboth, hboth, sems = refs[4:]
    high_half, low_half = pl.ds(0, D), pl.ds(D, D)
    hh, hlow = hboth.at[:, high_half], hboth.at[:, low_half]
    ph, plow = pboth.at[:, high_half], pboth.at[:, low_half]
    ph_in, plow_in, hh_in, hlow_in = kept(halves_in)
    steps = [pl.ds(i * STEP, STEP) for i in range(ROWS // STEP)]
    whole = [
        pltpu.make_async_copy(a, b, sems.at[k])
        for k, (a, b) in enumerate(((hh_in, hh), (hlow_in, hlow), (ph_in, ph), (plow_in, plow)))
    ]
    chunks = [
        pltpu.make_async_copy(expo_in.at[here, :], expo.at[here, :], sems.at[4 + i])
        for i, here in enumerate(steps)
    ]
    for copy in whole[:2] + chunks + whole[2:]:
        copy.start()
    x, y, c, zh, zl = (place[k] for k in range(5))
    first = c == 0
    scale = inv_temp / (2.0 * BATCH)
    rows = jnp.where(first, sums[...], other_sums[...])
    cols = jnp.where(first, other_sums[...], sums[...])
    row_term = jnp.sum(jnp.log(rows[:, :ROWS])) - 2.0 * jnp.sum(rows[:, ROWS:])
    col_term = jnp.sum(jnp.log(cols[:, : 2 * COLS]))
    row_inv = scale / rows[:, :ROWS]
    col_inv = scale / jnp.where(first, cols[:, :COLS], cols[:, COLS : 2 * COLS])
    places = ids[...]
    for copy in whole[:2]:
        copy.wait()
    for i, here in enumerate(steps):
        chunks[i].wait()
        per_row = jnp.concatenate(
            [to_rows(row_inv[:, k : k + 128]) for k in range(i * STEP, (i + 1) * STEP, 128)], axis=0
        )
        match = wanted[here, :] == places
        d = expo[here, :] * (per_row + col_inv) - jnp.where(match, 2.0 * scale, 0.0)
        high, low = split(d)
        dh[here, :] = high
        dlow[here, :] = low
        pgrads[here, :] = wide_product(high, low, hboth, 1)
    for copy in whole[2:]:
        copy.wait()
    for k in range(COLS // 128):
        here = pl.ds(k * 128, 128)
        hgrads[here, :] = wide_product(dh[:, here], dlow[:, here], pboth, 0)

    def at(outs, j):
        line = (3, 1, 2, 0)[j]
        return outs[line // 2].at[line % 2]

    def packets(outs, term):
        for j, k, core, block in row_blocks(x, zl):
            at(outs, j)[k, core * B : (core + 1) * B, :] = block_at(pgrads, block)[...]
        for j in range(4):
            at(outs, j)[:, 2 * B :, :] = jnp.zeros((4, 8, D), jnp.float32) + term

    def headers(outs, term, other):
        for j, k, block in col_blocks(y, zh, zl):
            at(outs, j)[k, other * B : (other + 1) * B, :] = block_at(hgrads, block)[...]
            at(outs, j)[k, (1 - other) * B : (2 - other) * B, :] = jnp.zeros((B, D), jnp.float32)
        for j in range(4):
            at(outs, j)[:, 2 * B :, :] = jnp.zeros((4, 8, D), jnp.float32) + term

    @pl.when(first)
    def _():
        packets(keeps, col_term)
        headers(sends, 0.0, 1)

    @pl.when(c == 1)
    def _():
        headers(keeps, row_term, 0)
        packets(sends, 0.0)


def last_kernel(place, packet, header, pair, got, packet_grad, header_grad, loss):
    first = place[2] == 0
    own, other = pair[:B, :], got[:B, :]

    def back(values, grads):
        norms = jnp.sqrt(jnp.sum(values * values, axis=1, keepdims=True) + eps_norm)
        inverse = 1.0 / norms
        units = values * inverse
        return (grads - units * jnp.sum(units * grads, axis=1, keepdims=True)) * inverse

    packet_grad[...] = back(packet[...], jnp.where(first, own, other))
    header_grad[...] = back(header[...], jnp.where(first, other, own))
    term = jnp.max(pair[2 * B :, :128] + got[B:, :128])
    loss[0, 0] = inv_temp + term / (2.0 * BATCH)


IN_VMEM = pl.BlockSpec(memory_space=pltpu.VMEM)
IN_SMEM = pl.BlockSpec(memory_space=pltpu.SMEM)
IN_PLACE = pl.BlockSpec(memory_space=pl.ANY)


def call(kernel, operands, in_specs, outs, out_specs, scratch, flops):
    return pl.pallas_call(
        kernel,
        in_specs=[IN_SMEM] + in_specs,
        out_specs=out_specs,
        out_shape=outs,
        scratch_shapes=scratch,
        compiler_params=pltpu.CompilerParams(vmem_limit_bytes=VMEM_LIMIT),
        cost_estimate=pl.CostEstimate(flops=flops, bytes_accessed=8 * 2**20, transcendentals=0),
    )(*operands)


def f32(*shape):
    return jax.ShapeDtypeStruct(shape, jnp.float32)


def b16(*shape):
    return jax.ShapeDtypeStruct(shape, jnp.bfloat16)


def together(*values):
    return lax.optimization_barrier(values)


def gather(first, packet, header):
    pair = jnp.concatenate(
        [
            jnp.where(first, packet, header),
            swap_core(jnp.where(first, header, packet)),
        ]
    )
    za = along_z(pair, 2, 1)
    zb = along_z(pair, 1, -1)
    line = jnp.stack([pair, za, zb, along_z(za, 1, 1)])
    ahead, behind = along_xy(line, 1), along_xy(line, -1)
    lines = [line, ahead, behind, along_xy(ahead, 1)]
    return lines, [swap_core(line) for line in lines]


def scatter(keeps, sends):
    far, ahead = (keeps[0] + swap_core(sends[0]))[:]
    behind, line = (keeps[1] + swap_core(sends[1]))[:]
    behind = jnp.concatenate([behind[:2] + along_xy(far[:2], 1), behind[2:]])
    ahead = jnp.concatenate([ahead[:2], ahead[2:] + along_xy(far[2:], -1)])
    line = line + along_xy(ahead, -1) + along_xy(behind, 1)
    za = line[1] + along_z(line[3], 1, -1)
    return line[0] + along_z(za, 2, -1) + along_z(line[2], 1, 1)


def per_device(packet, header, partner):
    x, y, c, zh, zl = (lax.axis_index(name) for name in ALL)
    place = jnp.stack([x, y, c, zh, zl]).astype(jnp.int32)
    lane = np.arange(COLS)
    ids = lane // (NY * B) * (NL * NX * NY * NC * B) + lane // B % NY * (NC * B) + lane % B
    ids = jnp.asarray(ids, jnp.int32)[None, :]
    ids = ids + ((zl * NX + x) * (NY * NC * B) + c * B).astype(jnp.int32)
    wanted = lax.dynamic_slice(
        partner.reshape(NX, NY, NC, NH, NL, B), [0, y, 0, zh, 0, 0], (NX, 1, NC, 1, NL, B)
    ).reshape(ROWS, 1)

    first = c == 0
    lines, other_lines = gather(first, packet, header)
    flops = 2 * 3 * ROWS * COLS * D
    tiles = [((ROWS, COLS), jnp.float32)] + [((ROWS, D), jnp.bfloat16)] * 2
    tiles += [((COLS, D), jnp.bfloat16)] * 2
    held = [pltpu.VMEM(*tile) for tile in tiles]
    expo, halves, keep, send = call(
        scores_kernel,
        [place, ids, wanted] + lines + other_lines,
        [IN_VMEM] * 10,
        [f32(KEPT_F32, COLS), b16(KEPT_B16, D), f32(1, SUMS), f32(1, SUMS)],
        [IN_PLACE] * 2 + [IN_VMEM] * 2,
        [pltpu.VMEM((ROWS, D), jnp.float32), pltpu.VMEM((COLS, D), jnp.float32), pltpu.VMEM((1, SUMS), jnp.float32)]
        + held
        + [pltpu.SemaphoreType.DMA((5,))],
        flops,
    )
    sums = lax.all_to_all(
        jnp.broadcast_to((keep + swap_core(send))[None], (16, 1, SUMS)),
        ALL, 0, 0, axis_index_groups=groups(),
    )
    sums = jnp.sum(sums, axis=0)
    parts = call(
        grads_kernel,
        [place, ids, wanted, sums, swap_core(sums), expo, halves],
        [IN_VMEM] * 4 + [IN_PLACE] * 2,
        [f32(2, 4, PAIR, D)] * 4,
        [IN_VMEM] * 4,
        [
            pltpu.VMEM((ROWS, COLS), jnp.bfloat16),
            pltpu.VMEM((ROWS, COLS), jnp.bfloat16),
            pltpu.VMEM((ROWS, D), jnp.float32),
            pltpu.VMEM((COLS, D), jnp.float32),
            pltpu.VMEM((ROWS, COLS), jnp.float32),
            pltpu.VMEM((ROWS, 2 * D), jnp.bfloat16),
            pltpu.VMEM((COLS, 2 * D), jnp.bfloat16),
            pltpu.SemaphoreType.DMA((4 + ROWS // STEP,)),
        ],
        2 * flops,
    )
    pair = scatter(parts[:2], parts[2:])
    packet_grad, header_grad, loss = call(
        last_kernel,
        [place, packet, header, pair, swap_core(pair[B:])],
        [IN_VMEM] * 4,
        [f32(B, D), f32(B, D), f32(1, 1)],
        [IN_VMEM, IN_VMEM, IN_SMEM],
        [],
        10 * B * D,
    )
    return (loss[0, 0], packet_grad, header_grad)


def solution(mesh):
    mesh = Mesh(mesh.devices.reshape(NX, NY, NC, NH, NL), ALL)
    by_packet, by_header = P(ALL, None), P(("zh", "zl", "x", "y", "core"), None)
    return jax.shard_map(
        per_device,
        mesh=mesh,
        in_specs=(by_packet, by_header, P()),
        out_specs=(P(), by_packet, by_header),
        check_vma=False,
    )
```

```python
import functools
import math

import jax
import jax.numpy as jnp
import numpy as np
from jax import lax
from jax.experimental import pallas as pl
from jax.experimental.pallas import tpu as pltpu
from jax.sharding import Mesh, PartitionSpec as P

inv_temp = 1.0 / 0.07
eps_norm = 1e-06
LOG2_SCALE = inv_temp * math.log2(math.e)
NX, NY, NC, NZ = 4, 4, 2, 16
NH, NL = 4, 4
ALL = ("x", "y", "core", "zh", "zl")
B = 40
D = 512
ROWS = NX * NC * NL * B
COLS = NY * NH * B
BATCH = NX * NY * NC * NZ * B
PAIR = 2 * B + 8
PLACES = (0, 1, -1, 2)
FLIPS = (0, 2, 1, 3)
VMEM_LIMIT = 48 * 2**20


def permute(value, source):
    pairs = []
    for x in range(NX):
        for y in range(NY):
            for c in range(NC):
                for z in range(NZ):
                    sx, sy, sc, sz = source(x, y, c, z)
                    src = (((sx % NX) * NY + sy % NY) * NC + sc) * NZ + sz
                    pairs.append((src, ((x * NY + y) * NC + c) * NZ + z))
    return lax.ppermute(value, ALL, pairs)


def along_xy(value, step):
    return permute(value, lambda x, y, c, z: (x + (1 - c) * step, y + c * step, c, z))


def along_z(value, flip, step):
    return permute(
        value,
        lambda x, y, c, z: (x, y, c, (z + NL * step * (1 - 2 * (z % 2))) % NZ if c else z ^ flip),
    )


def swap_core(value):
    return permute(value, lambda x, y, c, z: (x, y, c ^ 1, z))


def groups():
    index = np.arange(NX * NY * NC * NZ).reshape(NX, NY, NC, NH, NL)
    found = []
    for i in range(4):
        for j in range(4):
            found.append(index[:, i, 0, j, :].reshape(-1).tolist())
            found.append(index[i, :, 1, :, j].reshape(-1).tolist())
    return found


def row_blocks(x, zl):
    found = []
    for j, dx in enumerate(PLACES):
        bx = lax.rem(x + dx + NX, NX)
        for k, flip in enumerate(FLIPS):
            for core in range(NC):
                found.append((j, k, core, (bx * NC + core) * NL + (zl ^ flip)))
    return found


def col_blocks(y, zh, zl):
    found = []
    s = 1 - 2 * lax.rem(zl, 2)
    for j, dy in enumerate(PLACES):
        by = lax.rem(y + dy + NY, NY)
        for k, dz in enumerate(PLACES):
            found.append((j, k, lax.rem(zh + s * dz + NH, NH) * NY + by))
    return found


def block_at(ref, block):
    return ref.at[pl.ds(pl.multiple_of(block * B, 8), B), :]


def split(value):
    high = value.astype(jnp.bfloat16)
    return high, (value - high.astype(jnp.float32)).astype(jnp.bfloat16)


def product(a_high, a_low, b_high, b_low, dims):
    dot = functools.partial(
        lax.dot_general, dimension_numbers=(dims, ((), ())), preferred_element_type=jnp.float32
    )
    return dot(a_high, b_high) + (dot(a_high, b_low) + dot(a_low, b_high))


def wide_product(high, low, both, axis):
    dot = functools.partial(
        lax.dot_general,
        dimension_numbers=(((axis,), (0,)), ((), ())),
        preferred_element_type=jnp.float32,
    )
    wide = dot(high, both[...])
    return wide[:, :D] + (wide[:, D:] + dot(low, both[:, :D]))


def eye():
    return lax.broadcasted_iota(jnp.int32, (128, 128), 0) == lax.broadcasted_iota(
        jnp.int32, (128, 128), 1
    )


def to_lanes(column):
    return jnp.sum(jnp.where(eye(), column, 0.0), axis=0, keepdims=True)


def to_rows(lanes):
    return jnp.sum(jnp.where(eye(), lanes, 0.0), axis=1, keepdims=True)


STEP = 256
SUMS = ROWS + 128
KEPT_F32 = 6 * ROWS
KEPT_B16 = 16 * ROWS


def kept(whole):
    starts = (0, ROWS, 2 * ROWS, 2 * ROWS + COLS)
    return [whole.at[pl.ds(start, n), :] for start, n in zip(starts, (ROWS, ROWS, COLS, COLS))]


def scores_kernel(place, ids, wanted, *refs):
    mine, others = refs[:5], refs[5:10]
    expo_out, halves_out, keep, send = refs[10:14]
    punit, hunit, row_sums, expo, ph, plow, hh, hlow, sems = refs[14:]
    ph_out, plow_out, hh_out, hlow_out = kept(halves_out)
    x, y, c, zh, zl = (place[k] for k in range(5))

    def unit(v):
        return v * (1.0 / jnp.sqrt(jnp.sum(v * v, axis=1, keepdims=True) + eps_norm))

    def block_of(lines, j, k, half):
        pair = lines[j].at[k] if j < 3 else lines[3 + k // 2].at[k % 2]
        return pair[half * B : (half + 1) * B, :]

    def fill(rows_in, cols_in, other):
        for j, k, block in col_blocks(y, zh, zl):
            block_at(hunit, block)[...] = unit(block_of(cols_in, j, k, other))
        for j, k, core, block in row_blocks(x, zl):
            block_at(punit, block)[...] = unit(block_of(rows_in, j, k, core))

    @pl.when(c == 0)
    def _():
        fill(mine, others, 1)

    @pl.when(c == 1)
    def _():
        fill(others, mine, 0)

    hh[...], hlow[...] = split(hunit[...])
    turned_high, turned_low = split(hunit[...].T)
    whole = [
        pltpu.make_async_copy(hh, hh_out, sems.at[3]),
        pltpu.make_async_copy(hlow, hlow_out, sems.at[4]),
    ]
    for copy in whole:
        copy.start()
    places = ids[...]

    def copies(here):
        pairs = ((expo, expo_out), (ph, ph_out), (plow, plow_out))
        return [
            pltpu.make_async_copy(a.at[here, :], b.at[here, :], sems.at[k])
            for k, (a, b) in enumerate(pairs)
        ]

    total = positive = jnp.zeros((8, COLS), jnp.float32)
    for i in range(ROWS // STEP):
        here = pl.ds(i * STEP, STEP)
        high, low = split(punit[here, :])
        ph[here, :] = high
        plow[here, :] = low
        cosines = product(high, low, turned_high, turned_low, ((1,), (0,)))
        e = jnp.exp2(cosines * LOG2_SCALE - LOG2_SCALE)
        expo[here, :] = e
        if i:
            for copy in copies(pl.ds((i - 1) * STEP, STEP)):
                copy.wait()
        for copy in copies(here):
            copy.start()
        sums = jnp.sum(e, axis=1, keepdims=True)
        for k in range(0, STEP, 128):
            row_sums[:, pl.ds(i * STEP + k, 128)] = to_lanes(sums[k : k + 128])
        total = total + jnp.sum(e.reshape(STEP // 8, 8, COLS), axis=0)
        match = wanted[here, :] == places
        positive = positive + jnp.sum(
            jnp.where(match, cosines, 0.0).reshape(STEP // 8, 8, COLS), axis=0
        )

    for copy in copies(pl.ds(ROWS - STEP, STEP)) + whole:
        copy.wait()
    positive = jnp.sum(positive, axis=0, keepdims=True)
    row_sums[:, ROWS:] = inv_temp * sum(
        positive[:, k * 128 : (k + 1) * 128] for k in range(COLS // 128)
    )
    total = jnp.sum(total, axis=0, keepdims=True)
    none, rest = jnp.zeros_like(total), jnp.zeros((1, SUMS - ROWS), jnp.float32)

    @pl.when(c == 0)
    def _():
        keep[...] = row_sums[...]
        send[...] = jnp.concatenate([total, none, rest], axis=1)

    @pl.when(c == 1)
    def _():
        keep[...] = jnp.concatenate([none, total, rest], axis=1)
        send[...] = row_sums[...]


def grads_kernel(place, ids, wanted, sums, other_sums, expo_in, halves_in, *refs):
    keeps, sends = refs[:2], refs[2:4]
    dh, dlow, pgrads, hgrads, expo, pboth, hboth, sems = refs[4:]
    high_half, low_half = pl.ds(0, D), pl.ds(D, D)
    hh, hlow = hboth.at[:, high_half], hboth.at[:, low_half]
    ph, plow = pboth.at[:, high_half], pboth.at[:, low_half]
    ph_in, plow_in, hh_in, hlow_in = kept(halves_in)
    steps = [pl.ds(i * STEP, STEP) for i in range(ROWS // STEP)]
    whole = [
        pltpu.make_async_copy(a, b, sems.at[k])
        for k, (a, b) in enumerate(((hh_in, hh), (hlow_in, hlow), (ph_in, ph), (plow_in, plow)))
    ]
    chunks = [
        pltpu.make_async_copy(expo_in.at[here, :], expo.at[here, :], sems.at[4 + i])
        for i, here in enumerate(steps)
    ]
    for copy in whole[:2] + chunks + whole[2:]:
        copy.start()
    x, y, c, zh, zl = (place[k] for k in range(5))
    first = c == 0
    scale = inv_temp / (2.0 * BATCH)
    rows = jnp.where(first, sums[...], other_sums[...])
    cols = jnp.where(first, other_sums[...], sums[...])
    row_term = jnp.sum(jnp.log(rows[:, :ROWS])) - 2.0 * jnp.sum(rows[:, ROWS:])
    col_term = jnp.sum(jnp.log(cols[:, : 2 * COLS]))
    row_inv = scale / rows[:, :ROWS]
    col_inv = scale / jnp.where(first, cols[:, :COLS], cols[:, COLS : 2 * COLS])
    places = ids[...]
    for copy in whole[:2]:
        copy.wait()
    for i, here in enumerate(steps):
        chunks[i].wait()
        per_row = jnp.concatenate(
            [to_rows(row_inv[:, k : k + 128]) for k in range(i * STEP, (i + 1) * STEP, 128)], axis=0
        )
        match = wanted[here, :] == places
        d = expo[here, :] * (per_row + col_inv) - jnp.where(match, 2.0 * scale, 0.0)
        high, low = split(d)
        dh[here, :] = high
        dlow[here, :] = low
        pgrads[here, :] = wide_product(high, low, hboth, 1)
    for copy in whole[2:]:
        copy.wait()
    for k in range(COLS // 128):
        here = pl.ds(k * 128, 128)
        hgrads[here, :] = wide_product(dh[:, here], dlow[:, here], pboth, 0)

    def at(outs, j):
        line = (3, 1, 2, 0)[j]
        return outs[line // 2].at[line % 2]

    def packets(outs, term):
        for j, k, core, block in row_blocks(x, zl):
            at(outs, j)[k, core * B : (core + 1) * B, :] = block_at(pgrads, block)[...]
        for j in range(4):
            at(outs, j)[:, 2 * B :, :] = jnp.zeros((4, 8, D), jnp.float32) + term

    def headers(outs, term, other):
        for j, k, block in col_blocks(y, zh, zl):
            at(outs, j)[k, other * B : (other + 1) * B, :] = block_at(hgrads, block)[...]
            at(outs, j)[k, (1 - other) * B : (2 - other) * B, :] = jnp.zeros((B, D), jnp.float32)
        for j in range(4):
            at(outs, j)[:, 2 * B :, :] = jnp.zeros((4, 8, D), jnp.float32) + term

    @pl.when(first)
    def _():
        packets(keeps, col_term)
        headers(sends, 0.0, 1)

    @pl.when(c == 1)
    def _():
        headers(keeps, row_term, 0)
        packets(sends, 0.0)


def last_kernel(place, packet, header, pair, got, packet_grad, header_grad, loss):
    first = place[2] == 0
    own, other = pair[:B, :], got[:B, :]

    def back(values, grads):
        norms = jnp.sqrt(jnp.sum(values * values, axis=1, keepdims=True) + eps_norm)
        inverse = 1.0 / norms
        units = values * inverse
        return (grads - units * jnp.sum(units * grads, axis=1, keepdims=True)) * inverse

    packet_grad[...] = back(packet[...], jnp.where(first, own, other))
    header_grad[...] = back(header[...], jnp.where(first, other, own))
    term = jnp.max(pair[2 * B :, :128] + got[B:, :128])
    loss[0, 0] = inv_temp + term / (2.0 * BATCH)


IN_VMEM = pl.BlockSpec(memory_space=pltpu.VMEM)
IN_SMEM = pl.BlockSpec(memory_space=pltpu.SMEM)
IN_PLACE = pl.BlockSpec(memory_space=pl.ANY)


def call(kernel, operands, in_specs, outs, out_specs, scratch, flops):
    return pl.pallas_call(
        kernel,
        in_specs=[IN_SMEM] + in_specs,
        out_specs=out_specs,
        out_shape=outs,
        scratch_shapes=scratch,
        compiler_params=pltpu.CompilerParams(vmem_limit_bytes=VMEM_LIMIT),
        cost_estimate=pl.CostEstimate(flops=flops, bytes_accessed=8 * 2**20, transcendentals=0),
    )(*operands)


def f32(*shape):
    return jax.ShapeDtypeStruct(shape, jnp.float32)


def b16(*shape):
    return jax.ShapeDtypeStruct(shape, jnp.bfloat16)


def together(*values):
    return lax.optimization_barrier(values)


def gather(first, packet, header):
    pair = jnp.concatenate(
        [
            jnp.where(first, packet, header),
            swap_core(jnp.where(first, header, packet)),
        ]
    )
    za = along_z(pair, 2, 1)
    zb = along_z(pair, 1, -1)
    line = jnp.stack([pair, za, zb, along_z(za, 1, 1)])
    ahead, behind = along_xy(line, 1), along_xy(line, -1)
    lines = [line, ahead, behind, along_xy(ahead[:2], 1), along_xy(behind[2:], -1)]
    return lines, [swap_core(line) for line in lines]


def scatter(keeps, sends):
    far, ahead = (keeps[0] + swap_core(sends[0]))[:]
    behind, line = (keeps[1] + swap_core(sends[1]))[:]
    behind = jnp.concatenate([behind[:2] + along_xy(far[:2], 1), behind[2:]])
    ahead = jnp.concatenate([ahead[:2], ahead[2:] + along_xy(far[2:], -1)])
    line = line + along_xy(ahead, -1) + along_xy(behind, 1)
    za = line[1] + along_z(line[3], 1, -1)
    return line[0] + along_z(za, 2, -1) + along_z(line[2], 1, 1)


def per_device(packet, header, partner):
    x, y, c, zh, zl = (lax.axis_index(name) for name in ALL)
    place = jnp.stack([x, y, c, zh, zl]).astype(jnp.int32)
    lane = np.arange(COLS)
    ids = lane // (NY * B) * (NL * NX * NY * NC * B) + lane // B % NY * (NC * B) + lane % B
    ids = jnp.asarray(ids, jnp.int32)[None, :]
    ids = ids + ((zl * NX + x) * (NY * NC * B) + c * B).astype(jnp.int32)
    wanted = lax.dynamic_slice(
        partner.reshape(NX, NY, NC, NH, NL, B), [0, y, 0, zh, 0, 0], (NX, 1, NC, 1, NL, B)
    ).reshape(ROWS, 1)

    first = c == 0
    lines, other_lines = gather(first, packet, header)
    flops = 2 * 3 * ROWS * COLS * D
    tiles = [((ROWS, COLS), jnp.float32)] + [((ROWS, D), jnp.bfloat16)] * 2
    tiles += [((COLS, D), jnp.bfloat16)] * 2
    held = [pltpu.VMEM(*tile) for tile in tiles]
    expo, halves, keep, send = call(
        scores_kernel,
        [place, ids, wanted] + lines + other_lines,
        [IN_VMEM] * 12,
        [f32(KEPT_F32, COLS), b16(KEPT_B16, D), f32(1, SUMS), f32(1, SUMS)],
        [IN_PLACE] * 2 + [IN_VMEM] * 2,
        [pltpu.VMEM((ROWS, D), jnp.float32), pltpu.VMEM((COLS, D), jnp.float32), pltpu.VMEM((1, SUMS), jnp.float32)]
        + held
        + [pltpu.SemaphoreType.DMA((5,))],
        flops,
    )
    sums = lax.all_to_all(
        jnp.broadcast_to((keep + swap_core(send))[None], (16, 1, SUMS)),
        ALL, 0, 0, axis_index_groups=groups(),
    )
    sums = jnp.sum(sums, axis=0)
    parts = call(
        grads_kernel,
        [place, ids, wanted, sums, swap_core(sums), expo, halves],
        [IN_VMEM] * 4 + [IN_PLACE] * 2,
        [f32(2, 4, PAIR, D)] * 4,
        [IN_VMEM] * 4,
        [
            pltpu.VMEM((ROWS, COLS), jnp.bfloat16),
            pltpu.VMEM((ROWS, COLS), jnp.bfloat16),
            pltpu.VMEM((ROWS, D), jnp.float32),
            pltpu.VMEM((COLS, D), jnp.float32),
            pltpu.VMEM((ROWS, COLS), jnp.float32),
            pltpu.VMEM((ROWS, 2 * D), jnp.bfloat16),
            pltpu.VMEM((COLS, 2 * D), jnp.bfloat16),
            pltpu.SemaphoreType.DMA((4 + ROWS // STEP,)),
        ],
        2 * flops,
    )
    pair = scatter(parts[:2], parts[2:])
    packet_grad, header_grad, loss = call(
        last_kernel,
        [place, packet, header, pair, swap_core(pair[B:])],
        [IN_VMEM] * 4,
        [f32(B, D), f32(B, D), f32(1, 1)],
        [IN_VMEM, IN_VMEM, IN_SMEM],
        [],
        10 * B * D,
    )
    return (loss[0, 0], packet_grad, header_grad)


def solution(mesh):
    mesh = Mesh(mesh.devices.reshape(NX, NY, NC, NH, NL), ALL)
    by_packet, by_header = P(ALL, None), P(("zh", "zl", "x", "y", "core"), None)
    return jax.shard_map(
        per_device,
        mesh=mesh,
        in_specs=(by_packet, by_header, P()),
        out_specs=(P(), by_packet, by_header),
        check_vma=False,
    )
```

```python
import functools
import math

import jax
import jax.numpy as jnp
import numpy as np
from jax import lax
from jax.experimental import pallas as pl
from jax.experimental.pallas import tpu as pltpu
from jax.sharding import Mesh, PartitionSpec as P

inv_temp = 1.0 / 0.07
eps_norm = 1e-06
LOG2_SCALE = inv_temp * math.log2(math.e)
NX, NY, NC, NZ = 4, 4, 2, 16
NH, NL = 4, 4
ALL = ("x", "y", "core", "zh", "zl")
B = 40
D = 512
ROWS = NX * NC * NL * B
COLS = NY * NH * B
BATCH = NX * NY * NC * NZ * B
PAIR = 2 * B + 8
PLACES = (0, 1, -1, 2)
FLIPS = (0, 2, 1, 3)
VMEM_LIMIT = 48 * 2**20


def permute(value, source):
    pairs = []
    for x in range(NX):
        for y in range(NY):
            for c in range(NC):
                for z in range(NZ):
                    sx, sy, sc, sz = source(x, y, c, z)
                    src = (((sx % NX) * NY + sy % NY) * NC + sc) * NZ + sz
                    pairs.append((src, ((x * NY + y) * NC + c) * NZ + z))
    return lax.ppermute(value, ALL, pairs)


def along_xy(value, step):
    return permute(value, lambda x, y, c, z: (x + (1 - c) * step, y + c * step, c, z))


def along_z(value, flip, step):
    return permute(
        value,
        lambda x, y, c, z: (x, y, c, (z + NL * step * (1 - 2 * (z % 2))) % NZ if c else z ^ flip),
    )


def swap_core(value):
    return permute(value, lambda x, y, c, z: (x, y, c ^ 1, z))


def groups():
    index = np.arange(NX * NY * NC * NZ).reshape(NX, NY, NC, NH, NL)
    found = []
    for i in range(4):
        for j in range(4):
            found.append(index[:, i, 0, j, :].reshape(-1).tolist())
            found.append(index[i, :, 1, :, j].reshape(-1).tolist())
    return found


def row_blocks(x, zl):
    found = []
    for j, dx in enumerate(PLACES):
        bx = lax.rem(x + dx + NX, NX)
        for k, flip in enumerate(FLIPS):
            for core in range(NC):
                found.append((j, k, core, (bx * NC + core) * NL + (zl ^ flip)))
    return found


def col_blocks(y, zh, zl):
    found = []
    s = 1 - 2 * lax.rem(zl, 2)
    for j, dy in enumerate(PLACES):
        by = lax.rem(y + dy + NY, NY)
        for k, dz in enumerate(PLACES):
            found.append((j, k, lax.rem(zh + s * dz + NH, NH) * NY + by))
    return found


def block_at(ref, block):
    return ref.at[pl.ds(pl.multiple_of(block * B, 8), B), :]


def split(value):
    high = value.astype(jnp.bfloat16)
    return high, (value - high.astype(jnp.float32)).astype(jnp.bfloat16)


def product(a_high, a_low, b_high, b_low, dims):
    dot = functools.partial(
        lax.dot_general, dimension_numbers=(dims, ((), ())), preferred_element_type=jnp.float32
    )
    return dot(a_high, b_high) + (dot(a_high, b_low) + dot(a_low, b_high))


def wide_product(high, low, both, axis):
    dot = functools.partial(
        lax.dot_general,
        dimension_numbers=(((axis,), (0,)), ((), ())),
        preferred_element_type=jnp.float32,
    )
    wide = dot(high, both[...])
    return wide[:, :D] + (wide[:, D:] + dot(low, both[:, :D]))


def eye():
    return lax.broadcasted_iota(jnp.int32, (128, 128), 0) == lax.broadcasted_iota(
        jnp.int32, (128, 128), 1
    )


def to_lanes(column):
    return jnp.sum(jnp.where(eye(), column, 0.0), axis=0, keepdims=True)


def to_rows(lanes):
    return jnp.sum(jnp.where(eye(), lanes, 0.0), axis=1, keepdims=True)


STEP = 640
SUMS = ROWS + 128
KEPT_F32 = 6 * ROWS
KEPT_B16 = 16 * ROWS


def kept(whole):
    starts = (0, ROWS, 2 * ROWS, 2 * ROWS + COLS)
    return [whole.at[pl.ds(start, n), :] for start, n in zip(starts, (ROWS, ROWS, COLS, COLS))]


def scores_kernel(place, ids, wanted, *refs):
    mine, others = refs[:4], refs[4:8]
    expo_out, halves_out, keep, send = refs[8:12]
    punit, hunit, row_sums, expo, ph, plow, hh, hlow, sems = refs[12:]
    ph_out, plow_out, hh_out, hlow_out = kept(halves_out)
    x, y, c, zh, zl = (place[k] for k in range(5))

    def unit(v):
        return v * (1.0 / jnp.sqrt(jnp.sum(v * v, axis=1, keepdims=True) + eps_norm))

    def fill(rows_in, cols_in, other):
        for j, k, block in col_blocks(y, zh, zl):
            block_at(hunit, block)[...] = unit(cols_in[j][k, other * B : (other + 1) * B, :])
        for j, k, core, block in row_blocks(x, zl):
            block_at(punit, block)[...] = unit(rows_in[j][k, core * B : (core + 1) * B, :])

    @pl.when(c == 0)
    def _():
        fill(mine, others, 1)

    @pl.when(c == 1)
    def _():
        fill(others, mine, 0)

    hh[...], hlow[...] = split(hunit[...])
    turned_high, turned_low = split(hunit[...].T)
    whole = [
        pltpu.make_async_copy(hh, hh_out, sems.at[3]),
        pltpu.make_async_copy(hlow, hlow_out, sems.at[4]),
    ]
    for copy in whole:
        copy.start()
    places = ids[...]

    def copies(here):
        pairs = ((expo, expo_out), (ph, ph_out), (plow, plow_out))
        return [
            pltpu.make_async_copy(a.at[here, :], b.at[here, :], sems.at[k])
            for k, (a, b) in enumerate(pairs)
        ]

    total = positive = jnp.zeros((8, COLS), jnp.float32)
    for i in range(ROWS // STEP):
        here = pl.ds(i * STEP, STEP)
        high, low = split(punit[here, :])
        ph[here, :] = high
        plow[here, :] = low
        cosines = product(high, low, turned_high, turned_low, ((1,), (0,)))
        e = jnp.exp2(cosines * LOG2_SCALE - LOG2_SCALE)
        expo[here, :] = e
        if i:
            for copy in copies(pl.ds((i - 1) * STEP, STEP)):
                copy.wait()
        for copy in copies(here):
            copy.start()
        sums = jnp.sum(e, axis=1, keepdims=True)
        for k in range(0, STEP, 128):
            row_sums[:, pl.ds(i * STEP + k, 128)] = to_lanes(sums[k : k + 128])
        total = total + jnp.sum(e.reshape(STEP // 8, 8, COLS), axis=0)
        match = wanted[here, :] == places
        positive = positive + jnp.sum(
            jnp.where(match, cosines, 0.0).reshape(STEP // 8, 8, COLS), axis=0
        )

    for copy in copies(pl.ds(ROWS - STEP, STEP)) + whole:
        copy.wait()
    positive = jnp.sum(positive, axis=0, keepdims=True)
    row_sums[:, ROWS:] = inv_temp * sum(
        positive[:, k * 128 : (k + 1) * 128] for k in range(COLS // 128)
    )
    total = jnp.sum(total, axis=0, keepdims=True)
    none, rest = jnp.zeros_like(total), jnp.zeros((1, SUMS - ROWS), jnp.float32)

    @pl.when(c == 0)
    def _():
        keep[...] = row_sums[...]
        send[...] = jnp.concatenate([total, none, rest], axis=1)

    @pl.when(c == 1)
    def _():
        keep[...] = jnp.concatenate([none, total, rest], axis=1)
        send[...] = row_sums[...]


def grads_kernel(place, ids, wanted, sums, other_sums, expo_in, halves_in, *refs):
    keeps, sends = refs[:2], refs[2:4]
    dh, dlow, pgrads, hgrads, expo, pboth, hboth, sems = refs[4:]
    high_half, low_half = pl.ds(0, D), pl.ds(D, D)
    hh, hlow = hboth.at[:, high_half], hboth.at[:, low_half]
    ph, plow = pboth.at[:, high_half], pboth.at[:, low_half]
    ph_in, plow_in, hh_in, hlow_in = kept(halves_in)
    steps = [pl.ds(i * STEP, STEP) for i in range(ROWS // STEP)]
    whole = [
        pltpu.make_async_copy(a, b, sems.at[k])
        for k, (a, b) in enumerate(((hh_in, hh), (hlow_in, hlow), (ph_in, ph), (plow_in, plow)))
    ]
    chunks = [
        pltpu.make_async_copy(expo_in.at[here, :], expo.at[here, :], sems.at[4 + i])
        for i, here in enumerate(steps)
    ]
    for copy in whole[:2] + chunks + whole[2:]:
        copy.start()
    x, y, c, zh, zl = (place[k] for k in range(5))
    first = c == 0
    scale = inv_temp / (2.0 * BATCH)
    rows = jnp.where(first, sums[...], other_sums[...])
    cols = jnp.where(first, other_sums[...], sums[...])
    row_term = jnp.sum(jnp.log(rows[:, :ROWS])) - 2.0 * jnp.sum(rows[:, ROWS:])
    col_term = jnp.sum(jnp.log(cols[:, : 2 * COLS]))
    row_inv = scale / rows[:, :ROWS]
    col_inv = scale / jnp.where(first, cols[:, :COLS], cols[:, COLS : 2 * COLS])
    places = ids[...]
    for copy in whole[:2]:
        copy.wait()
    for i, here in enumerate(steps):
        chunks[i].wait()
        per_row = jnp.concatenate(
            [to_rows(row_inv[:, k : k + 128]) for k in range(i * STEP, (i + 1) * STEP, 128)], axis=0
        )
        match = wanted[here, :] == places
        d = expo[here, :] * (per_row + col_inv) - jnp.where(match, 2.0 * scale, 0.0)
        high, low = split(d)
        dh[here, :] = high
        dlow[here, :] = low
        pgrads[here, :] = wide_product(high, low, hboth, 1)
    for copy in whole[2:]:
        copy.wait()
    hgrads[...] = wide_product(dh[...], dlow[...], pboth, 0)

    def at(outs, j):
        line = (3, 1, 2, 0)[j]
        return outs[line // 2].at[line % 2]

    def packets(outs, term):
        for j, k, core, block in row_blocks(x, zl):
            at(outs, j)[k, core * B : (core + 1) * B, :] = block_at(pgrads, block)[...]
        for j in range(4):
            at(outs, j)[:, 2 * B :, :] = jnp.zeros((4, 8, D), jnp.float32) + term

    def headers(outs, term, other):
        for j, k, block in col_blocks(y, zh, zl):
            at(outs, j)[k, other * B : (other + 1) * B, :] = block_at(hgrads, block)[...]
            at(outs, j)[k, (1 - other) * B : (2 - other) * B, :] = jnp.zeros((B, D), jnp.float32)
        for j in range(4):
            at(outs, j)[:, 2 * B :, :] = jnp.zeros((4, 8, D), jnp.float32) + term

    @pl.when(first)
    def _():
        packets(keeps, col_term)
        headers(sends, 0.0, 1)

    @pl.when(c == 1)
    def _():
        headers(keeps, row_term, 0)
        packets(sends, 0.0)


def last_kernel(place, packet, header, pair, got, packet_grad, header_grad, loss):
    first = place[2] == 0
    own, other = pair[:B, :], got[:B, :]

    def back(values, grads):
        norms = jnp.sqrt(jnp.sum(values * values, axis=1, keepdims=True) + eps_norm)
        inverse = 1.0 / norms
        units = values * inverse
        return (grads - units * jnp.sum(units * grads, axis=1, keepdims=True)) * inverse

    packet_grad[...] = back(packet[...], jnp.where(first, own, other))
    header_grad[...] = back(header[...], jnp.where(first, other, own))
    term = jnp.max(pair[2 * B :, :128] + got[B:, :128])
    loss[0, 0] = inv_temp + term / (2.0 * BATCH)


IN_VMEM = pl.BlockSpec(memory_space=pltpu.VMEM)
IN_SMEM = pl.BlockSpec(memory_space=pltpu.SMEM)
IN_PLACE = pl.BlockSpec(memory_space=pl.ANY)


def call(kernel, operands, in_specs, outs, out_specs, scratch, flops):
    return pl.pallas_call(
        kernel,
        in_specs=[IN_SMEM] + in_specs,
        out_specs=out_specs,
        out_shape=outs,
        scratch_shapes=scratch,
        compiler_params=pltpu.CompilerParams(vmem_limit_bytes=VMEM_LIMIT),
        cost_estimate=pl.CostEstimate(flops=flops, bytes_accessed=8 * 2**20, transcendentals=0),
    )(*operands)


def f32(*shape):
    return jax.ShapeDtypeStruct(shape, jnp.float32)


def b16(*shape):
    return jax.ShapeDtypeStruct(shape, jnp.bfloat16)


def together(*values):
    return lax.optimization_barrier(values)


def gather(first, packet, header):
    pair = jnp.concatenate(
        [
            jnp.where(first, packet, header),
            swap_core(jnp.where(first, header, packet)),
        ]
    )
    za = along_z(pair, 2, 1)
    zb = along_z(pair, 1, -1)
    line = jnp.stack([pair, za, zb, along_z(za, 1, 1)])
    ahead, behind = along_xy(line, 1), along_xy(line, -1)
    lines = [line, ahead, behind, along_xy(ahead, 1)]
    return lines, [swap_core(line) for line in lines]


def scatter(keeps, sends):
    far, ahead = (keeps[0] + swap_core(sends[0]))[:]
    behind, line = (keeps[1] + swap_core(sends[1]))[:]
    behind = jnp.concatenate([behind[:2] + along_xy(far[:2], 1), behind[2:]])
    ahead = jnp.concatenate([ahead[:2], ahead[2:] + along_xy(far[2:], -1)])
    line = line + along_xy(ahead, -1) + along_xy(behind, 1)
    za = line[1] + along_z(line[3], 1, -1)
    return line[0] + along_z(za, 2, -1) + along_z(line[2], 1, 1)


def per_device(packet, header, partner):
    x, y, c, zh, zl = (lax.axis_index(name) for name in ALL)
    place = jnp.stack([x, y, c, zh, zl]).astype(jnp.int32)
    lane = np.arange(COLS)
    ids = lane // (NY * B) * (NL * NX * NY * NC * B) + lane // B % NY * (NC * B) + lane % B
    ids = jnp.asarray(ids, jnp.int32)[None, :]
    ids = ids + ((zl * NX + x) * (NY * NC * B) + c * B).astype(jnp.int32)
    wanted = lax.dynamic_slice(
        partner.reshape(NX, NY, NC, NH, NL, B), [0, y, 0, zh, 0, 0], (NX, 1, NC, 1, NL, B)
    ).reshape(ROWS, 1)

    first = c == 0
    lines, other_lines = gather(first, packet, header)
    flops = 2 * 3 * ROWS * COLS * D
    tiles = [((ROWS, COLS), jnp.float32)] + [((ROWS, D), jnp.bfloat16)] * 2
    tiles += [((COLS, D), jnp.bfloat16)] * 2
    held = [pltpu.VMEM(*tile) for tile in tiles]
    expo, halves, keep, send = call(
        scores_kernel,
        [place, ids, wanted] + lines + other_lines,
        [IN_VMEM] * 10,
        [f32(KEPT_F32, COLS), b16(KEPT_B16, D), f32(1, SUMS), f32(1, SUMS)],
        [IN_PLACE] * 2 + [IN_VMEM] * 2,
        [pltpu.VMEM((ROWS, D), jnp.float32), pltpu.VMEM((COLS, D), jnp.float32), pltpu.VMEM((1, SUMS), jnp.float32)]
        + held
        + [pltpu.SemaphoreType.DMA((5,))],
        flops,
    )
    sums = lax.all_to_all(
        jnp.broadcast_to((keep + swap_core(send))[None], (16, 1, SUMS)),
        ALL, 0, 0, axis_index_groups=groups(),
    )
    sums = jnp.sum(sums, axis=0)
    parts = call(
        grads_kernel,
        [place, ids, wanted, sums, swap_core(sums), expo, halves],
        [IN_VMEM] * 4 + [IN_PLACE] * 2,
        [f32(2, 4, PAIR, D)] * 4,
        [IN_VMEM] * 4,
        [
            pltpu.VMEM((ROWS, COLS), jnp.bfloat16),
            pltpu.VMEM((ROWS, COLS), jnp.bfloat16),
            pltpu.VMEM((ROWS, D), jnp.float32),
            pltpu.VMEM((COLS, D), jnp.float32),
            pltpu.VMEM((ROWS, COLS), jnp.float32),
            pltpu.VMEM((ROWS, 2 * D), jnp.bfloat16),
            pltpu.VMEM((COLS, 2 * D), jnp.bfloat16),
            pltpu.SemaphoreType.DMA((4 + ROWS // STEP,)),
        ],
        2 * flops,
    )
    pair = scatter(parts[:2], parts[2:])
    packet_grad, header_grad, loss = call(
        last_kernel,
        [place, packet, header, pair, swap_core(pair[B:])],
        [IN_VMEM] * 4,
        [f32(B, D), f32(B, D), f32(1, 1)],
        [IN_VMEM, IN_VMEM, IN_SMEM],
        [],
        10 * B * D,
    )
    return (loss[0, 0], packet_grad, header_grad)


def solution(mesh):
    mesh = Mesh(mesh.devices.reshape(NX, NY, NC, NH, NL), ALL)
    by_packet, by_header = P(ALL, None), P(("zh", "zl", "x", "y", "core"), None)
    return jax.shard_map(
        per_device,
        mesh=mesh,
        in_specs=(by_packet, by_header, P()),
        out_specs=(P(), by_packet, by_header),
        check_vma=False,
    )
```

```python
import functools
import math

import jax
import jax.numpy as jnp
import numpy as np
from jax import lax
from jax.experimental import pallas as pl
from jax.experimental.pallas import tpu as pltpu
from jax.sharding import Mesh, PartitionSpec as P

inv_temp = 1.0 / 0.07
eps_norm = 1e-06
LOG2_SCALE = inv_temp * math.log2(math.e)
NX, NY, NC, NZ = 4, 4, 2, 16
NH, NL = 4, 4
ALL = ("x", "y", "core", "zh", "zl")
B = 40
D = 512
ROWS = NX * NC * NL * B
COLS = NY * NH * B
BATCH = NX * NY * NC * NZ * B
PAIR = 2 * B + 8
PLACES = (0, 1, -1, 2)
FLIPS = (0, 2, 1, 3)
VMEM_LIMIT = 48 * 2**20


def permute(value, source):
    pairs = []
    for x in range(NX):
        for y in range(NY):
            for c in range(NC):
                for z in range(NZ):
                    sx, sy, sc, sz = source(x, y, c, z)
                    src = (((sx % NX) * NY + sy % NY) * NC + sc) * NZ + sz
                    pairs.append((src, ((x * NY + y) * NC + c) * NZ + z))
    return lax.ppermute(value, ALL, pairs)


def along_xy(value, step):
    return permute(value, lambda x, y, c, z: (x + (1 - c) * step, y + c * step, c, z))


def along_z(value, flip, step):
    return permute(
        value,
        lambda x, y, c, z: (x, y, c, (z + NL * step * (1 - 2 * (z % 2))) % NZ if c else z ^ flip),
    )


def swap_core(value):
    return permute(value, lambda x, y, c, z: (x, y, c ^ 1, z))


def groups():
    index = np.arange(NX * NY * NC * NZ).reshape(NX, NY, NC, NH, NL)
    found = []
    for i in range(4):
        for j in range(4):
            found.append(index[:, i, 0, j, :].reshape(-1).tolist())
            found.append(index[i, :, 1, :, j].reshape(-1).tolist())
    return found


def row_blocks(x, zl):
    found = []
    for j, dx in enumerate(PLACES):
        bx = lax.rem(x + dx + NX, NX)
        for k, flip in enumerate(FLIPS):
            for core in range(NC):
                found.append((j, k, core, (bx * NC + core) * NL + (zl ^ flip)))
    return found


def col_blocks(y, zh, zl):
    found = []
    s = 1 - 2 * lax.rem(zl, 2)
    for j, dy in enumerate(PLACES):
        by = lax.rem(y + dy + NY, NY)
        for k, dz in enumerate(PLACES):
            found.append((j, k, lax.rem(zh + s * dz + NH, NH) * NY + by))
    return found


def block_at(ref, block):
    return ref.at[pl.ds(pl.multiple_of(block * B, 8), B), :]


def split(value):
    high = value.astype(jnp.bfloat16)
    return high, (value - high.astype(jnp.float32)).astype(jnp.bfloat16)


def product(a_high, a_low, b_high, b_low, dims):
    dot = functools.partial(
        lax.dot_general, dimension_numbers=(dims, ((), ())), preferred_element_type=jnp.float32
    )
    return dot(a_high, b_high) + (dot(a_high, b_low) + dot(a_low, b_high))


def wide_product(high, low, both, axis):
    dot = functools.partial(
        lax.dot_general,
        dimension_numbers=(((axis,), (0,)), ((), ())),
        preferred_element_type=jnp.float32,
    )
    wide = dot(high, both[...])
    return wide[:, :D] + (wide[:, D:] + dot(low, both[:, :D]))


def eye():
    return lax.broadcasted_iota(jnp.int32, (128, 128), 0) == lax.broadcasted_iota(
        jnp.int32, (128, 128), 1
    )


def to_lanes(column):
    return jnp.sum(jnp.where(eye(), column, 0.0), axis=0, keepdims=True)


def to_rows(lanes):
    return jnp.sum(jnp.where(eye(), lanes, 0.0), axis=1, keepdims=True)


STEP = 640
SUMS = ROWS + 128
KEPT_F32 = 6 * ROWS
KEPT_B16 = 16 * ROWS


def kept(whole):
    starts = (0, ROWS, 2 * ROWS, 2 * ROWS + COLS)
    return [whole.at[pl.ds(start, n), :] for start, n in zip(starts, (ROWS, ROWS, COLS, COLS))]


def scores_kernel(place, ids, wanted, *refs):
    mine, others = refs[:4], refs[4:8]
    expo_out, halves_out, keep, send = refs[8:12]
    punit, hunit, row_sums, expo, ph, plow, hh, hlow, sems = refs[12:]
    ph_out, plow_out, hh_out, hlow_out = kept(halves_out)
    x, y, c, zh, zl = (place[k] for k in range(5))

    def unit(v):
        return v * (1.0 / jnp.sqrt(jnp.sum(v * v, axis=1, keepdims=True) + eps_norm))

    def fill(rows_in, cols_in, other):
        for j, k, block in col_blocks(y, zh, zl):
            block_at(hunit, block)[...] = cols_in[j][k, other * B : (other + 1) * B, :]
        for j, k, core, block in row_blocks(x, zl):
            block_at(punit, block)[...] = rows_in[j][k, core * B : (core + 1) * B, :]

    @pl.when(c == 0)
    def _():
        fill(mine, others, 1)

    @pl.when(c == 1)
    def _():
        fill(others, mine, 0)

    hunit[...] = unit(hunit[...])
    hh[...], hlow[...] = split(hunit[...])
    turned_high, turned_low = split(hunit[...].T)
    whole = [
        pltpu.make_async_copy(hh, hh_out, sems.at[3]),
        pltpu.make_async_copy(hlow, hlow_out, sems.at[4]),
    ]
    for copy in whole:
        copy.start()
    places = ids[...]

    def copies(here):
        pairs = ((expo, expo_out), (ph, ph_out), (plow, plow_out))
        return [
            pltpu.make_async_copy(a.at[here, :], b.at[here, :], sems.at[k])
            for k, (a, b) in enumerate(pairs)
        ]

    total = positive = jnp.zeros((8, COLS), jnp.float32)
    for i in range(ROWS // STEP):
        here = pl.ds(i * STEP, STEP)
        high, low = split(unit(punit[here, :]))
        ph[here, :] = high
        plow[here, :] = low
        cosines = product(high, low, turned_high, turned_low, ((1,), (0,)))
        e = jnp.exp2(cosines * LOG2_SCALE - LOG2_SCALE)
        expo[here, :] = e
        if i:
            for copy in copies(pl.ds((i - 1) * STEP, STEP)):
                copy.wait()
        for copy in copies(here):
            copy.start()
        sums = jnp.sum(e, axis=1, keepdims=True)
        for k in range(0, STEP, 128):
            row_sums[:, pl.ds(i * STEP + k, 128)] = to_lanes(sums[k : k + 128])
        total = total + jnp.sum(e.reshape(STEP // 8, 8, COLS), axis=0)
        match = wanted[here, :] == places
        positive = positive + jnp.sum(
            jnp.where(match, cosines, 0.0).reshape(STEP // 8, 8, COLS), axis=0
        )

    for copy in copies(pl.ds(ROWS - STEP, STEP)) + whole:
        copy.wait()
    positive = jnp.sum(positive, axis=0, keepdims=True)
    row_sums[:, ROWS:] = inv_temp * sum(
        positive[:, k * 128 : (k + 1) * 128] for k in range(COLS // 128)
    )
    total = jnp.sum(total, axis=0, keepdims=True)
    none, rest = jnp.zeros_like(total), jnp.zeros((1, SUMS - ROWS), jnp.float32)

    @pl.when(c == 0)
    def _():
        keep[...] = row_sums[...]
        send[...] = jnp.concatenate([total, none, rest], axis=1)

    @pl.when(c == 1)
    def _():
        keep[...] = jnp.concatenate([none, total, rest], axis=1)
        send[...] = row_sums[...]


def grads_kernel(place, ids, wanted, sums, other_sums, expo_in, halves_in, *refs):
    keeps, sends = refs[:2], refs[2:4]
    dh, dlow, pgrads, hgrads, expo, pboth, hboth, sems = refs[4:]
    high_half, low_half = pl.ds(0, D), pl.ds(D, D)
    hh, hlow = hboth.at[:, high_half], hboth.at[:, low_half]
    ph, plow = pboth.at[:, high_half], pboth.at[:, low_half]
    ph_in, plow_in, hh_in, hlow_in = kept(halves_in)
    steps = [pl.ds(i * STEP, STEP) for i in range(ROWS // STEP)]
    whole = [
        pltpu.make_async_copy(a, b, sems.at[k])
        for k, (a, b) in enumerate(((hh_in, hh), (hlow_in, hlow), (ph_in, ph), (plow_in, plow)))
    ]
    chunks = [
        pltpu.make_async_copy(expo_in.at[here, :], expo.at[here, :], sems.at[4 + i])
        for i, here in enumerate(steps)
    ]
    for copy in whole[:2] + chunks + whole[2:]:
        copy.start()
    x, y, c, zh, zl = (place[k] for k in range(5))
    first = c == 0
    scale = inv_temp / (2.0 * BATCH)
    rows = jnp.where(first, sums[...], other_sums[...])
    cols = jnp.where(first, other_sums[...], sums[...])
    row_term = jnp.sum(jnp.log(rows[:, :ROWS])) - 2.0 * jnp.sum(rows[:, ROWS:])
    col_term = jnp.sum(jnp.log(cols[:, : 2 * COLS]))
    row_inv = scale / rows[:, :ROWS]
    col_inv = scale / jnp.where(first, cols[:, :COLS], cols[:, COLS : 2 * COLS])
    places = ids[...]
    for copy in whole[:2]:
        copy.wait()
    for i, here in enumerate(steps):
        chunks[i].wait()
        per_row = jnp.concatenate(
            [to_rows(row_inv[:, k : k + 128]) for k in range(i * STEP, (i + 1) * STEP, 128)], axis=0
        )
        match = wanted[here, :] == places
        d = expo[here, :] * (per_row + col_inv) - jnp.where(match, 2.0 * scale, 0.0)
        high, low = split(d)
        dh[here, :] = high
        dlow[here, :] = low
        pgrads[here, :] = wide_product(high, low, hboth, 1)
    for copy in whole[2:]:
        copy.wait()
    hgrads[...] = wide_product(dh[...], dlow[...], pboth, 0)

    def at(outs, j):
        line = (3, 1, 2, 0)[j]
        return outs[line // 2].at[line % 2]

    def packets(outs, term):
        for j, k, core, block in row_blocks(x, zl):
            at(outs, j)[k, core * B : (core + 1) * B, :] = block_at(pgrads, block)[...]
        for j in range(4):
            at(outs, j)[:, 2 * B :, :] = jnp.zeros((4, 8, D), jnp.float32) + term

    def headers(outs, term, other):
        for j, k, block in col_blocks(y, zh, zl):
            at(outs, j)[k, other * B : (other + 1) * B, :] = block_at(hgrads, block)[...]
            at(outs, j)[k, (1 - other) * B : (2 - other) * B, :] = jnp.zeros((B, D), jnp.float32)
        for j in range(4):
            at(outs, j)[:, 2 * B :, :] = jnp.zeros((4, 8, D), jnp.float32) + term

    @pl.when(first)
    def _():
        packets(keeps, col_term)
        headers(sends, 0.0, 1)

    @pl.when(c == 1)
    def _():
        headers(keeps, row_term, 0)
        packets(sends, 0.0)


def last_kernel(place, packet, header, pair, got, packet_grad, header_grad, loss):
    first = place[2] == 0
    own, other = pair[:B, :], got[:B, :]

    def back(values, grads):
        norms = jnp.sqrt(jnp.sum(values * values, axis=1, keepdims=True) + eps_norm)
        inverse = 1.0 / norms
        units = values * inverse
        return (grads - units * jnp.sum(units * grads, axis=1, keepdims=True)) * inverse

    packet_grad[...] = back(packet[...], jnp.where(first, own, other))
    header_grad[...] = back(header[...], jnp.where(first, other, own))
    term = jnp.max(pair[2 * B :, :128] + got[B:, :128])
    loss[0, 0] = inv_temp + term / (2.0 * BATCH)


IN_VMEM = pl.BlockSpec(memory_space=pltpu.VMEM)
IN_SMEM = pl.BlockSpec(memory_space=pltpu.SMEM)
IN_PLACE = pl.BlockSpec(memory_space=pl.ANY)


def call(kernel, operands, in_specs, outs, out_specs, scratch, flops):
    return pl.pallas_call(
        kernel,
        in_specs=[IN_SMEM] + in_specs,
        out_specs=out_specs,
        out_shape=outs,
        scratch_shapes=scratch,
        compiler_params=pltpu.CompilerParams(vmem_limit_bytes=VMEM_LIMIT),
        cost_estimate=pl.CostEstimate(flops=flops, bytes_accessed=8 * 2**20, transcendentals=0),
    )(*operands)


def f32(*shape):
    return jax.ShapeDtypeStruct(shape, jnp.float32)


def b16(*shape):
    return jax.ShapeDtypeStruct(shape, jnp.bfloat16)


def together(*values):
    return lax.optimization_barrier(values)


def gather(first, packet, header):
    pair = jnp.concatenate(
        [
            jnp.where(first, packet, header),
            swap_core(jnp.where(first, header, packet)),
        ]
    )
    za = along_z(pair, 2, 1)
    zb = along_z(pair, 1, -1)
    line = jnp.stack([pair, za, zb, along_z(za, 1, 1)])
    ahead, behind = along_xy(line, 1), along_xy(line, -1)
    lines = [line, ahead, behind, along_xy(ahead, 1)]
    return lines, [swap_core(line) for line in lines]


def scatter(keeps, sends):
    far, ahead = (keeps[0] + swap_core(sends[0]))[:]
    behind, line = (keeps[1] + swap_core(sends[1]))[:]
    behind = jnp.concatenate([behind[:2] + along_xy(far[:2], 1), behind[2:]])
    ahead = jnp.concatenate([ahead[:2], ahead[2:] + along_xy(far[2:], -1)])
    line = line + along_xy(ahead, -1) + along_xy(behind, 1)
    za = line[1] + along_z(line[3], 1, -1)
    return line[0] + along_z(za, 2, -1) + along_z(line[2], 1, 1)


def per_device(packet, header, partner):
    x, y, c, zh, zl = (lax.axis_index(name) for name in ALL)
    place = jnp.stack([x, y, c, zh, zl]).astype(jnp.int32)
    lane = np.arange(COLS)
    ids = lane // (NY * B) * (NL * NX * NY * NC * B) + lane // B % NY * (NC * B) + lane % B
    ids = jnp.asarray(ids, jnp.int32)[None, :]
    ids = ids + ((zl * NX + x) * (NY * NC * B) + c * B).astype(jnp.int32)
    wanted = lax.dynamic_slice(
        partner.reshape(NX, NY, NC, NH, NL, B), [0, y, 0, zh, 0, 0], (NX, 1, NC, 1, NL, B)
    ).reshape(ROWS, 1)

    first = c == 0
    lines, other_lines = gather(first, packet, header)
    flops = 2 * 3 * ROWS * COLS * D
    tiles = [((ROWS, COLS), jnp.float32)] + [((ROWS, D), jnp.bfloat16)] * 2
    tiles += [((COLS, D), jnp.bfloat16)] * 2
    held = [pltpu.VMEM(*tile) for tile in tiles]
    expo, halves, keep, send = call(
        scores_kernel,
        [place, ids, wanted] + lines + other_lines,
        [IN_VMEM] * 10,
        [f32(KEPT_F32, COLS), b16(KEPT_B16, D), f32(1, SUMS), f32(1, SUMS)],
        [IN_PLACE] * 2 + [IN_VMEM] * 2,
        [pltpu.VMEM((ROWS, D), jnp.float32), pltpu.VMEM((COLS, D), jnp.float32), pltpu.VMEM((1, SUMS), jnp.float32)]
        + held
        + [pltpu.SemaphoreType.DMA((5,))],
        flops,
    )
    sums = lax.all_to_all(
        jnp.broadcast_to((keep + swap_core(send))[None], (16, 1, SUMS)),
        ALL, 0, 0, axis_index_groups=groups(),
    )
    sums = jnp.sum(sums, axis=0)
    parts = call(
        grads_kernel,
        [place, ids, wanted, sums, swap_core(sums), expo, halves],
        [IN_VMEM] * 4 + [IN_PLACE] * 2,
        [f32(2, 4, PAIR, D)] * 4,
        [IN_VMEM] * 4,
        [
            pltpu.VMEM((ROWS, COLS), jnp.bfloat16),
            pltpu.VMEM((ROWS, COLS), jnp.bfloat16),
            pltpu.VMEM((ROWS, D), jnp.float32),
            pltpu.VMEM((COLS, D), jnp.float32),
            pltpu.VMEM((ROWS, COLS), jnp.float32),
            pltpu.VMEM((ROWS, 2 * D), jnp.bfloat16),
            pltpu.VMEM((COLS, 2 * D), jnp.bfloat16),
            pltpu.SemaphoreType.DMA((4 + ROWS // STEP,)),
        ],
        2 * flops,
    )
    pair = scatter(parts[:2], parts[2:])
    packet_grad, header_grad, loss = call(
        last_kernel,
        [place, packet, header, pair, swap_core(pair[B:])],
        [IN_VMEM] * 4,
        [f32(B, D), f32(B, D), f32(1, 1)],
        [IN_VMEM, IN_VMEM, IN_SMEM],
        [],
        10 * B * D,
    )
    return (loss[0, 0], packet_grad, header_grad)


def solution(mesh):
    mesh = Mesh(mesh.devices.reshape(NX, NY, NC, NH, NL), ALL)
    by_packet, by_header = P(ALL, None), P(("zh", "zl", "x", "y", "core"), None)
    return jax.shard_map(
        per_device,
        mesh=mesh,
        in_specs=(by_packet, by_header, P()),
        out_specs=(P(), by_packet, by_header),
        check_vma=False,
    )
```
